256 devices in a mesh: context: 32 (over z_lo, x, core), tensor: 8 (over y, z_hi).
Axes of the slice: x: 4, y: 4, z: 8 (z_hi: 2, z_lo: 4; z = z_hi * 4 + z_lo), core: 2. Of those that a mesh axis runs over, the one named last changes fastest.
Arguments:
- q_gate: bfloat16 [8192, 4096], P('context', 'tensor'), may hold values from -6 to 6
- k_gate: bfloat16 [8192, 4096], P('context', 'tensor'), may hold values from -6 to 6
- v_input: bfloat16 [8192, 4096], P('context', 'tensor'), may hold values from -6 to 6
- filter_taps: bfloat16 [8192, 4096], P('context', 'tensor'), may hold values from -6 to 6
- skip_bias: float32 [4096], P('tensor'), may hold values from -4 to 4
- out_grad: bfloat16 [8192, 4096], P('context', 'tensor'), may hold values from -6 to 6
Outputs:
- mixed: bfloat16 [8192, 4096], P('context', 'tensor')
- q_grad: bfloat16 [8192, 4096], P('context', 'tensor')
- k_grad: bfloat16 [8192, 4096], P('context', 'tensor')
- v_grad: bfloat16 [8192, 4096], P('context', 'tensor')
- filter_grad: bfloat16 [8192, 4096], P('context', 'tensor')
The draws below stay inside these ranges and needn't reach their ends.
All inputs are finite; a program needn't handle non-finite values.
Results may differ from the reference program's by a relative error of at most 0.013.
Values may be sent and summed in bfloat16 or wider, within the bound.
No kernel may reach another device: no remote copies, remote signals or barrier semaphores. Data moves between devices by JAX's collectives and lax.ppermute only.
A program may use at most 64 MiB of HBM per device.

```python
import jax
import jax.numpy as jnp
from jax import lax

D = 4096
SEQ = 8192
NFFT = 16384


def steps_of(rng, dims, shards, smallest, top_value):
    def one(dim, blocks):
        draws = jax.random.uniform(jax.random.fold_in(jax.random.fold_in(rng, 6), dim), (blocks,), jnp.float32, smallest / len(shards), top_value / len(shards))
        return jnp.repeat(jnp.exp(draws), dims[dim] // blocks).reshape((-1,) + (1,) * (len(dims) - dim - 1))

    level = one(*shards[0])
    for cut in shards[1:]:
        level = level * one(*cut)
    return level


def gaussian(rng, extent, spread, limit, shards=(), held_as=jnp.bfloat16):
    gain = steps_of(rng, extent, shards, -0.22, 0.18) if shards else 1.0
    result = jax.random.normal(rng, extent, jnp.float32) * spread * gain
    return jnp.minimum(jnp.maximum(result, -limit), limit).astype(held_as)


def setup_inputs(seed: int = 0) -> dict:
    splits = jax.random.split(jax.random.key(seed), 7)
    q_gate = gaussian(splits[0], (SEQ, D), 1.0, 6.0, ((0, 32), (1, 8)))
    k_gate = gaussian(splits[1], (SEQ, D), 1.0, 6.0, ((0, 32), (1, 8)))
    v_input = gaussian(splits[2], (SEQ, D), 1.0, 6.0, ((0, 32), (1, 8)))
    filter_taps = gaussian(splits[3], (SEQ, D), 1.0, 6.0, ((0, 32), (1, 8)))
    skip_bias = gaussian(splits[4], (D,), 1.0, 4.0, ((0, 8),), jnp.float32)
    out_grad = gaussian(splits[5], (SEQ, D), 1.0, 6.0, ((0, 32), (1, 8)))
    return {"q_gate": q_gate, "k_gate": k_gate, "v_input": v_input, "filter_taps": filter_taps, "skip_bias": skip_bias, "out_grad": out_grad}


def reference(q_gate, k_gate, v_input, filter_taps, skip_bias, out_grad):
    gated = (k_gate * v_input).astype(jnp.bfloat16)
    delta = (out_grad * q_gate).astype(jnp.bfloat16)
    width = min(D, 256)
    blocks = D // width
    scale = 1.0 / jnp.sqrt(jnp.float32(SEQ))

    def to_blocks(arr):
        return arr.reshape(SEQ, blocks, width).transpose(1, 0, 2)

    def channel_block(pieces):
        g_part, f_part, d_part = pieces
        g_spec = jnp.fft.rfft(g_part.astype(jnp.float32), n=NFFT, axis=0)
        f_spec = jnp.fft.rfft(f_part.astype(jnp.float32), n=NFFT, axis=0)
        d_spec = jnp.fft.rfft(d_part.astype(jnp.float32), n=NFFT, axis=0)
        conv = jnp.fft.irfft(g_spec * f_spec, n=NFFT, axis=0)[:SEQ] * scale
        back = jnp.fft.irfft(jnp.conj(f_spec) * d_spec, n=NFFT, axis=0)[:SEQ] * scale
        fgrad = jnp.fft.irfft(jnp.conj(g_spec) * d_spec, n=NFFT, axis=0)[:SEQ] * scale
        return (conv.astype(jnp.bfloat16), back.astype(jnp.bfloat16), fgrad.astype(jnp.bfloat16))
    conv_b, back_b, fgrad_b = lax.map(channel_block, (to_blocks(gated), to_blocks(filter_taps), to_blocks(delta)))

    def from_blocks(arr):
        return arr.transpose(1, 0, 2).reshape(SEQ, D)
    conv_term = from_blocks(conv_b).astype(jnp.float32)
    back_term = from_blocks(back_b).astype(jnp.float32)
    filter_grad = from_blocks(fgrad_b)
    gated_f = gated.astype(jnp.float32)
    delta_f = delta.astype(jnp.float32)
    pre_gate = conv_term + skip_bias[None, :] * gated_f
    mixed = (q_gate.astype(jnp.float32) * pre_gate).astype(jnp.bfloat16)
    q_grad = (out_grad.astype(jnp.float32) * pre_gate).astype(jnp.bfloat16)
    gated_grad = back_term + skip_bias[None, :] * delta_f
    k_grad = (gated_grad * v_input.astype(jnp.float32)).astype(jnp.bfloat16)
    v_grad = (gated_grad * k_gate.astype(jnp.float32)).astype(jnp.bfloat16)
    return (mixed, q_grad, k_grad, v_grad, filter_grad)
```

```python
import functools
import math

import jax
import jax.numpy as jnp
import ml_dtypes
import numpy as np
from jax import lax
from jax.experimental import pallas as pl
from jax.experimental.pallas import tpu as pltpu
from jax.sharding import PartitionSpec as P

BF16 = jnp.bfloat16
F32 = jnp.float32


def make_tables(groups, rows, chans):
    length = 2 * groups * rows
    a = np.arange(groups)[None, :]
    b = np.arange(rows)[None, :]
    half = np.arange(groups)[:, None] + 0.5
    theta = 2.0 * math.pi * a * half / (2 * groups)
    eye = np.eye(chans)
    first = np.concatenate([np.kron(np.cos(theta), eye), np.kron(-np.sin(theta), eye)], axis=0)
    k2 = np.arange(rows)[:, None]
    phi = 2.0 * math.pi * ((k2 * b) % rows) / rows
    second = np.block([[np.cos(phi), -np.sin(phi)], [np.sin(phi), np.cos(phi)]])
    psi = 2.0 * math.pi * b * half / length
    low = ml_dtypes.bfloat16
    return (
        first.astype(low),
        np.ascontiguousarray(first.T).astype(low),
        second.astype(low),
        np.ascontiguousarray(second.T).astype(low),
        np.cos(psi).astype(np.float32)[:, None, :],
        (-np.sin(psi)).astype(np.float32)[:, None, :],
    )


def prep_kernel(q_ref, k_ref, v_ref, f_ref, og_ref, out_ref):
    owners, three, rows = out_ref.shape
    chans = three // 3

    def put(slot, block):
        out_ref[:, slot * chans : (slot + 1) * chans, :] = block.T.reshape(owners, chans, rows)

    put(0, k_ref[...] * v_ref[...])
    put(1, f_ref[...])
    put(2, og_ref[...] * q_ref[...])


def dot(a, b):
    return jnp.dot(a, b, preferred_element_type=F32)


def core_kernel(scale, x_ref, first_ref, first_t_ref, second_ref, second_t_ref, twr_ref, twi_ref, y_ref):
    groups, three, rows = x_ref.shape
    chans = three // 3
    lines = groups * chans
    twr, twi = twr_ref[...], twi_ref[...]

    def split3(block):
        return block.reshape(groups, chans, rows)

    def spectrum(slot):
        block = x_ref[:, slot * chans : (slot + 1) * chans, :].reshape(lines, rows)
        part = dot(first_ref[...], block)
        real, imag = split3(part[:lines]), split3(part[lines:])
        turned_real = (real * twr - imag * twi).astype(BF16).reshape(lines, rows)
        turned_imag = (real * twi + imag * twr).astype(BF16).reshape(lines, rows)
        out = dot(jnp.concatenate([turned_real, turned_imag], axis=1), second_ref[...])
        return out[:, :rows], out[:, rows:]

    def signal(real, imag, slot):
        joined = jnp.concatenate([real.astype(BF16), imag.astype(BF16)], axis=1)
        back = dot(joined, second_t_ref[...])
        real, imag = split3(back[:, :rows]), split3(back[:, rows:])
        turned_real = (real * twr + imag * twi).astype(BF16).reshape(lines, rows)
        turned_imag = (imag * twr - real * twi).astype(BF16).reshape(lines, rows)
        out = dot(first_t_ref[...], jnp.concatenate([turned_real, turned_imag], axis=0))
        y_ref[:, slot * chans : (slot + 1) * chans, :] = split3((out * scale).astype(BF16))

    gr, gi = spectrum(0)
    fr, fi = spectrum(1)
    signal(gr * fr - gi * fi, gr * fi + gi * fr, 0)
    dr, di = spectrum(2)
    signal(fr * dr + fi * di, fr * di - fi * dr, 1)
    signal(gr * dr + gi * di, gr * di - gi * dr, 2)


def post_kernel(y_ref, q_ref, k_ref, v_ref, og_ref, bias_ref, mixed_ref, qg_ref, kg_ref, vg_ref, fg_ref):
    owners, three, rows = y_ref.shape
    chans = three // 3

    def take(slot):
        return y_ref[:, slot * chans : (slot + 1) * chans, :].reshape(owners * chans, rows).T

    q, k, v, og = q_ref[...], k_ref[...], v_ref[...], og_ref[...]
    bias = bias_ref[...]
    q32, og32 = q.astype(F32), og.astype(F32)
    pre_gate = take(0).astype(F32) + bias * (k * v).astype(F32)
    mixed_ref[...] = (q32 * pre_gate).astype(BF16)
    qg_ref[...] = (og32 * pre_gate).astype(BF16)
    gated_grad = take(1).astype(F32) + bias * (og * q).astype(F32)
    kg_ref[...] = (gated_grad * v.astype(F32)).astype(BF16)
    vg_ref[...] = (gated_grad * k.astype(F32)).astype(BF16)
    fg_ref[...] = take(2)


def local(q_gate, k_gate, v_input, filter_taps, skip_bias, out_grad):
    groups = lax.axis_size("context")
    rows, width = q_gate.shape
    chans = width // groups
    tables = make_tables(groups, rows, chans)
    seq = groups * rows
    scale = 2.0 / (2 * seq) / math.sqrt(seq)
    steps = 4
    cols = width // steps
    owners = groups // steps
    tile = pl.BlockSpec((rows, cols), lambda i: (0, i))
    message = pl.BlockSpec((owners, 3 * chans, rows), lambda i: (i, 0, 0))
    messages = jax.ShapeDtypeStruct((groups, 3 * chans, rows), BF16)
    whole = jax.ShapeDtypeStruct((rows, width), BF16)
    limit = pltpu.CompilerParams(vmem_limit_bytes=48 * 1024 * 1024)

    sent = pl.pallas_call(
        prep_kernel, grid=(steps,), in_specs=[tile] * 5, out_specs=message, out_shape=messages, compiler_params=limit
    )(q_gate, k_gate, v_input, filter_taps, out_grad)
    items = lax.all_to_all(sent, "context", split_axis=0, concat_axis=0, tiled=True)
    terms = pl.pallas_call(
        functools.partial(core_kernel, scale), out_shape=messages, compiler_params=limit
    )(items, *tables)
    back = lax.all_to_all(terms, "context", split_axis=0, concat_axis=0, tiled=True)
    return pl.pallas_call(
        post_kernel,
        grid=(steps,),
        in_specs=[message] + [tile] * 4 + [pl.BlockSpec((1, cols), lambda i: (0, i))],
        out_specs=[tile] * 5,
        out_shape=[whole] * 5,
        compiler_params=limit,
    )(back, q_gate, k_gate, v_input, out_grad, skip_bias[None, :])


def solution(mesh):
    spec = P("context", "tensor")
    return jax.shard_map(
        local,
        mesh=mesh,
        in_specs=(spec, spec, spec, spec, P("tensor"), spec),
        out_specs=(spec,) * 5,
        check_vma=False,
    )
```

```python
import functools
import math

import jax
import jax.numpy as jnp
import ml_dtypes
import numpy as np
from jax import lax
from jax.experimental import pallas as pl
from jax.experimental.pallas import tpu as pltpu
from jax.sharding import PartitionSpec as P

BF16 = jnp.bfloat16
F32 = jnp.float32


def device_order(groups):
    quarter = groups // 4
    ids = list(range(groups))
    return ids[quarter : 2 * quarter] + ids[:quarter] + ids[2 * quarter :]


def make_tables(order, rows):
    groups = len(order)
    length = 2 * groups * rows
    a = np.array(order)[None, :]
    b = np.arange(rows)[None, :]
    half = np.arange(groups)[:, None] + 0.5
    theta = 2.0 * math.pi * a * half / (2 * groups)
    first = np.concatenate([np.cos(theta), -np.sin(theta)], axis=0)
    psi = 2.0 * math.pi * b * half / length
    low = np.arange(rows // 2)[:, None]
    m = np.arange(rows // 2)[None, :]
    second = []
    for parity in (0, 1):
        phi = 2.0 * math.pi * ((low * (2 * m + parity)) % rows) / rows
        second.append(np.block([[np.cos(phi), -np.sin(phi)], [np.sin(phi), np.cos(phi)]]))
    second = np.stack(second)
    narrow = ml_dtypes.bfloat16
    return (
        first.astype(narrow),
        np.ascontiguousarray(first.T).astype(narrow),
        second.astype(narrow),
        np.ascontiguousarray(second.transpose(0, 2, 1)).astype(narrow),
        np.cos(psi).astype(np.float32),
        (-np.sin(psi)).astype(np.float32),
    )


def prep_kernel(f_hbm, k_hbm, v_hbm, q_hbm, og_hbm, out_ref, held, sems):
    owners, three, rows = out_ref.shape
    chans = three // 3
    copies = [
        pltpu.make_async_copy(src, held.at[i], sems.at[i]) for i, src in enumerate((f_hbm, k_hbm, v_hbm, q_hbm, og_hbm))
    ]
    for copy in copies:
        copy.start()

    def put(slot, block):
        out_ref[:, slot * chans : (slot + 1) * chans, :] = block.T.reshape(owners, chans, rows)

    copies[0].wait()
    put(1, held[0])
    copies[1].wait()
    copies[2].wait()
    put(0, held[1] * held[2])
    copies[3].wait()
    copies[4].wait()
    put(2, held[3] * held[4])


def dot(a, b):
    return jnp.dot(a, b, preferred_element_type=F32)


def core_kernel(scale, x_ref, first_ref, first_t_ref, second_ref, second_t_ref, twr_ref, twi_ref, y_ref, t_ref, v_ref):
    groups, three, rows = x_ref.shape
    chans = three // 3
    h = rows // 2
    twr, twi = twr_ref[...], twi_ref[...]
    for s in range(3):
        items = jnp.swapaxes(x_ref[:, s * chans : (s + 1) * chans, :], 0, 1)
        for c in range(chans):
            part = dot(first_ref[...], items[c])
            real, imag = part[:groups], part[groups:]
            tr, ti = real * twr - imag * twi, real * twi + imag * twr
            lines = slice(c * groups, (c + 1) * groups)
            t_ref[s, 0, lines, :h] = (tr[:, :h] + tr[:, h:]).astype(BF16)
            t_ref[s, 0, lines, h:] = (ti[:, :h] + ti[:, h:]).astype(BF16)
            t_ref[s, 1, lines, :h] = (tr[:, :h] - tr[:, h:]).astype(BF16)
            t_ref[s, 1, lines, h:] = (ti[:, :h] - ti[:, h:]).astype(BF16)
    halves = []
    for parity in (0, 1):
        g, f, d = (dot(t_ref[s, parity], second_ref[parity]) for s in range(3))
        gr, gi, fr, fi, dr, di = g[:, :h], g[:, h:], f[:, :h], f[:, h:], d[:, :h], d[:, h:]
        products = (
            (gr * fr - gi * fi, gr * fi + gi * fr),
            (fr * dr + fi * di, fr * di - fi * dr),
            (gr * dr + gi * di, gr * di - gi * dr),
        )
        halves.append(
            [
                dot(jnp.concatenate([real.astype(BF16), imag.astype(BF16)], axis=1), second_t_ref[parity])
                for real, imag in products
            ]
        )
    for s in range(3):
        even, odd = (half[s].reshape(chans, groups, rows) for half in halves)
        for part, lanes in ((even + odd, slice(0, h)), (even - odd, slice(h, rows))):
            real, imag = part[:, :, :h], part[:, :, h:]
            v_ref[s, :, :groups, lanes] = (real * twr[:, lanes] + imag * twi[:, lanes]).astype(BF16)
            v_ref[s, :, groups:, lanes] = (imag * twr[:, lanes] - real * twi[:, lanes]).astype(BF16)
    for s in range(3):
        out = jnp.stack([dot(first_t_ref[...], v_ref[s, c]) * scale for c in range(chans)], axis=0)
        y_ref[:, s * chans : (s + 1) * chans, :] = jnp.swapaxes(out.astype(BF16), 0, 1)


def post_kernel(y_ref, q_ref, k_ref, v_ref, og_ref, bias_ref, mixed_hbm, qg_hbm, kg_hbm, vg_hbm, fg_hbm, held, sems):
    owners, three, rows = y_ref.shape
    chans = three // 3
    parts = held.shape[1]
    step = rows // parts
    bias = bias_ref[...]
    outs = (fg_hbm, mixed_hbm, qg_hbm, kg_hbm, vg_hbm)
    copies = []

    def put(i, p, block):
        held[i, p] = block.astype(BF16)
        copy = pltpu.make_async_copy(held.at[i, p], outs[i].at[pl.ds(p * step, step)], sems.at[i, p])
        copy.start()
        copies.append(copy)

    for p in range(parts):
        span = slice(p * step, (p + 1) * step)

        def take(slot):
            return y_ref[:, slot * chans : (slot + 1) * chans, span].reshape(owners * chans, step).T

        put(0, p, take(2))
        q, k, v, og = q_ref[span], k_ref[span], v_ref[span], og_ref[span]
        pre_gate = take(0).astype(F32) + bias * (k * v).astype(F32)
        put(1, p, q.astype(F32) * pre_gate)
        put(2, p, og.astype(F32) * pre_gate)
        gated_grad = take(1).astype(F32) + bias * (og * q).astype(F32)
        put(3, p, gated_grad * v.astype(F32))
        put(4, p, gated_grad * k.astype(F32))
    for copy in copies:
        copy.wait()


def local(q_gate, k_gate, v_input, filter_taps, skip_bias, out_grad):
    groups = lax.axis_size("context")
    rows, width = q_gate.shape
    chans = width // groups
    order = device_order(groups)
    seq = groups * rows
    scale = 2.0 / (2 * seq) / math.sqrt(seq)
    messages = jax.ShapeDtypeStruct((groups, 3 * chans, rows), BF16)
    whole = jax.ShapeDtypeStruct((rows, width), BF16)
    limit = pltpu.CompilerParams(vmem_limit_bytes=48 * 1024 * 1024)
    far = pl.BlockSpec(memory_space=pltpu.HBM)
    near = pl.BlockSpec(memory_space=pltpu.VMEM)

    def swap(block):
        return lax.all_to_all(
            block, "context", split_axis=0, concat_axis=0, tiled=True, axis_index_groups=[order]
        )

    sent = pl.pallas_call(
        prep_kernel,
        in_specs=[far] * 5,
        out_specs=near,
        out_shape=messages,
        scratch_shapes=[pltpu.VMEM((5, rows, width), BF16), pltpu.SemaphoreType.DMA((5,))],
        name="gate_and_pack",
    )(filter_taps, k_gate, v_input, q_gate, out_grad)
    terms = pl.pallas_call(
        functools.partial(core_kernel, scale),
        out_shape=messages,
        scratch_shapes=[
            pltpu.VMEM((3, 2, chans * groups, rows), BF16),
            pltpu.VMEM((3, chans, 2 * groups, rows), BF16),
        ],
        compiler_params=limit,
        name="transforms",
    )(swap(sent), *make_tables(order, rows))
    parts = 2
    return pl.pallas_call(
        post_kernel,
        in_specs=[near] * 6,
        out_specs=[far] * 5,
        out_shape=[whole] * 5,
        scratch_shapes=[
            pltpu.VMEM((5, parts, rows // parts, width), BF16),
            pltpu.SemaphoreType.DMA((5, parts)),
        ],
        compiler_params=limit,
        name="unpack_and_gate",
    )(swap(terms), q_gate, k_gate, v_input, out_grad, skip_bias[None, :])


def solution(mesh):
    spec = P("context", "tensor")
    return jax.shard_map(
        local,
        mesh=mesh,
        in_specs=(spec, spec, spec, spec, P("tensor"), spec),
        out_specs=(spec,) * 5,
        check_vma=False,
    )
```

```python
import functools
import math

import jax
import jax.numpy as jnp
import ml_dtypes
import numpy as np
from jax import lax
from jax.experimental import pallas as pl
from jax.experimental.pallas import tpu as pltpu
from jax.sharding import PartitionSpec as P

BF16 = jnp.bfloat16
F32 = jnp.float32


def device_order(groups):
    quarter = groups // 4
    ids = list(range(groups))
    return ids[quarter : 2 * quarter] + ids[:quarter] + ids[2 * quarter :]


def make_tables(order, rows):
    groups = len(order)
    length = 2 * groups * rows
    a = np.array(order)[None, :]
    b = np.arange(rows)[None, :]
    half = np.arange(groups)[:, None] + 0.5
    theta = 2.0 * math.pi * a * half / (2 * groups)
    first = np.concatenate([np.cos(theta), -np.sin(theta)], axis=0)
    psi = 2.0 * math.pi * b * half / length
    low = np.arange(rows // 2)[:, None]
    m = np.arange(rows // 2)[None, :]
    second = []
    for parity in (0, 1):
        phi = 2.0 * math.pi * ((low * (2 * m + parity)) % rows) / rows
        second.append(np.block([[np.cos(phi), -np.sin(phi)], [np.sin(phi), np.cos(phi)]]))
    second = np.stack(second)
    narrow = ml_dtypes.bfloat16
    return (
        first.astype(narrow),
        np.ascontiguousarray(first.T).astype(narrow),
        second.astype(narrow),
        np.ascontiguousarray(second.transpose(0, 2, 1)).astype(narrow),
        np.cos(psi).astype(np.float32),
        (-np.sin(psi)).astype(np.float32),
    )


def prep_kernel(f_hbm, k_hbm, v_hbm, q_hbm, og_hbm, out_ref, held, sems):
    owners, three, rows = out_ref.shape
    chans = three // 3
    copies = [
        pltpu.make_async_copy(src, held.at[i], sems.at[i]) for i, src in enumerate((f_hbm, k_hbm, v_hbm, q_hbm, og_hbm))
    ]
    for copy in copies:
        copy.start()

    def put(slot, block):
        out_ref[:, slot * chans : (slot + 1) * chans, :] = block.T.reshape(owners, chans, rows)

    copies[0].wait()
    put(1, held[0])
    copies[1].wait()
    copies[2].wait()
    put(0, held[1] * held[2])
    copies[3].wait()
    copies[4].wait()
    put(2, held[3] * held[4])


def dot(a, b):
    return jnp.dot(a, b, preferred_element_type=F32)


def core_kernel(scale, x_ref, first_ref, first_t_ref, second_ref, second_t_ref, twr_ref, twi_ref, y_ref, t_ref, v_ref):
    groups, three, rows = x_ref.shape
    chans = three // 3
    h = rows // 2
    twr, twi = twr_ref[...], twi_ref[...]
    for s in range(3):
        items = jnp.swapaxes(x_ref[:, s * chans : (s + 1) * chans, :], 0, 1)
        for c in range(chans):
            part = dot(first_ref[...], items[c])
            real, imag = part[:groups], part[groups:]
            tr, ti = real * twr - imag * twi, real * twi + imag * twr
            lines = slice(c * groups, (c + 1) * groups)
            t_ref[s, 0, lines, :h] = (tr[:, :h] + tr[:, h:]).astype(BF16)
            t_ref[s, 0, lines, h:] = (ti[:, :h] + ti[:, h:]).astype(BF16)
            t_ref[s, 1, lines, :h] = (tr[:, :h] - tr[:, h:]).astype(BF16)
            t_ref[s, 1, lines, h:] = (ti[:, :h] - ti[:, h:]).astype(BF16)
    halves = []
    for parity in (0, 1):
        g, f, d = (dot(t_ref[s, parity], second_ref[parity]) for s in range(3))
        gr, gi, fr, fi, dr, di = g[:, :h], g[:, h:], f[:, :h], f[:, h:], d[:, :h], d[:, h:]
        products = (
            (gr * fr - gi * fi, gr * fi + gi * fr),
            (fr * dr + fi * di, fr * di - fi * dr),
            (gr * dr + gi * di, gr * di - gi * dr),
        )
        halves.append(
            [
                dot(jnp.concatenate([real.astype(BF16), imag.astype(BF16)], axis=1), second_t_ref[parity])
                for real, imag in products
            ]
        )
    for s in range(3):
        even, odd = (half[s].reshape(chans, groups, rows) for half in halves)
        for part, lanes in ((even + odd, slice(0, h)), (even - odd, slice(h, rows))):
            real, imag = part[:, :, :h], part[:, :, h:]
            v_ref[s, :, :groups, lanes] = (real * twr[:, lanes] + imag * twi[:, lanes]).astype(BF16)
            v_ref[s, :, groups:, lanes] = (imag * twr[:, lanes] - real * twi[:, lanes]).astype(BF16)
    for s in range(3):
        out = jnp.stack([dot(first_t_ref[...], v_ref[s, c]) * scale for c in range(chans)], axis=0)
        y_ref[:, s * chans : (s + 1) * chans, :] = jnp.swapaxes(out.astype(BF16), 0, 1)


def post_kernel(y_ref, q_ref, k_ref, v_ref, og_ref, bias_ref, mixed_hbm, qg_hbm, kg_hbm, vg_hbm, fg_hbm, held, sems):
    owners, three, rows = y_ref.shape
    chans = three // 3
    parts = held.shape[1]
    step = rows // parts
    bias = bias_ref[...]
    outs = (fg_hbm, mixed_hbm, qg_hbm, kg_hbm, vg_hbm)
    copies = []

    def put(i, p, block):
        held[i, p] = block.astype(BF16)
        copy = pltpu.make_async_copy(held.at[i, p], outs[i].at[pl.ds(p * step, step)], sems.at[i, p])
        copy.start()
        copies.append(copy)

    for p in range(parts):
        span = slice(p * step, (p + 1) * step)

        def take(slot):
            return y_ref[:, slot * chans : (slot + 1) * chans, span].reshape(owners * chans, step).T

        put(0, p, take(2))
        q, k, v, og = q_ref[span], k_ref[span], v_ref[span], og_ref[span]
        pre_gate = take(0).astype(F32) + bias * (k * v).astype(F32)
        put(1, p, q.astype(F32) * pre_gate)
        put(2, p, og.astype(F32) * pre_gate)
        gated_grad = take(1).astype(F32) + bias * (og * q).astype(F32)
        put(3, p, gated_grad * v.astype(F32))
        put(4, p, gated_grad * k.astype(F32))
    for copy in copies:
        copy.wait()


def local(q_gate, k_gate, v_input, filter_taps, skip_bias, out_grad):
    groups = lax.axis_size("context")
    rows, width = q_gate.shape
    chans = width // groups
    order = device_order(groups)
    seq = groups * rows
    scale = 2.0 / (2 * seq) / math.sqrt(seq)
    messages = jax.ShapeDtypeStruct((groups, 3 * chans, rows), BF16)
    whole = jax.ShapeDtypeStruct((rows, width), BF16)
    limit = pltpu.CompilerParams(vmem_limit_bytes=48 * 1024 * 1024)
    far = pl.BlockSpec(memory_space=pltpu.HBM)
    near = pl.BlockSpec(memory_space=pltpu.VMEM)

    def swap(block):
        return lax.all_to_all(
            block, "context", split_axis=0, concat_axis=0, tiled=True, axis_index_groups=[order]
        )

    sent = pl.pallas_call(
        prep_kernel,
        in_specs=[far] * 5,
        out_specs=near,
        out_shape=pltpu.VMEM(messages.shape, BF16),
        scratch_shapes=[pltpu.VMEM((5, rows, width), BF16), pltpu.SemaphoreType.DMA((5,))],
        compiler_params=limit,
        name="gate_and_pack",
    )(*(pltpu.with_memory_space_constraint(x, pltpu.HBM) for x in (filter_taps, k_gate, v_input, q_gate, out_grad)))
    terms = pl.pallas_call(
        functools.partial(core_kernel, scale),
        out_shape=messages,
        scratch_shapes=[
            pltpu.VMEM((3, 2, chans * groups, rows), BF16),
            pltpu.VMEM((3, chans, 2 * groups, rows), BF16),
        ],
        compiler_params=limit,
        name="transforms",
    )(swap(sent), *make_tables(order, rows))
    parts = 2
    return pl.pallas_call(
        post_kernel,
        in_specs=[near] * 6,
        out_specs=[far] * 5,
        out_shape=[whole] * 5,
        scratch_shapes=[
            pltpu.VMEM((5, parts, rows // parts, width), BF16),
            pltpu.SemaphoreType.DMA((5, parts)),
        ],
        compiler_params=limit,
        name="unpack_and_gate",
    )(swap(terms), q_gate, k_gate, v_input, out_grad, skip_bias[None, :])


def solution(mesh):
    spec = P("context", "tensor")
    return jax.shard_map(
        local,
        mesh=mesh,
        in_specs=(spec, spec, spec, spec, P("tensor"), spec),
        out_specs=(spec,) * 5,
        check_vma=False,
    )
```

```python
import functools
import math

import jax
import jax.numpy as jnp
import ml_dtypes
import numpy as np
from jax import lax
from jax.experimental import pallas as pl
from jax.experimental.pallas import tpu as pltpu
from jax.sharding import PartitionSpec as P

BF16 = jnp.bfloat16
F32 = jnp.float32
WEIGHT = 8 * 10**9


QUARTERS = 4


def place(here):
    along = 4
    return here // (2 * along), here // 2 % along, here % 2


def block_of(here, dz, dx, dc):
    z, x, c = place(here)
    z = z ^ dz
    return ((z ^ (1 - z // 2)) * 4 + (x + dx) % 4) * 2 + (c ^ dc)


def device_order(groups):
    return [block_of(here, 0, 0, 0) for here in range(groups)]


def send(block, dz, dx, dc):
    groups = lax.axis_size("context")
    order = device_order(groups)
    moves = [(here, order[block_of(here, dz, dx, dc)]) for here in range(groups)]
    return lax.ppermute(block, "context", moves)


def make_tables(order, rows):
    groups = len(order)
    length = 2 * groups * rows
    a = np.array(order)[None, :]
    b = np.arange(rows)[None, :]
    half = np.arange(groups)[:, None] + 0.5
    theta = 2.0 * math.pi * a * half / (2 * groups)
    first = np.concatenate([np.cos(theta), -np.sin(theta)], axis=0)
    psi = 2.0 * math.pi * b * half / length
    low = np.arange(rows // 2)[:, None]
    m = np.arange(rows // 2)[None, :]
    second = []
    for parity in (0, 1):
        phi = 2.0 * math.pi * ((low * (2 * m + parity)) % rows) / rows
        second.append(np.block([[np.cos(phi), -np.sin(phi)], [np.sin(phi), np.cos(phi)]]))
    second = np.stack(second)
    narrow = ml_dtypes.bfloat16
    return (
        first.astype(narrow),
        np.ascontiguousarray(first.T).astype(narrow),
        second.astype(narrow),
        np.ascontiguousarray(second.transpose(0, 2, 1)).astype(narrow),
        np.cos(psi).astype(np.float32),
        (-np.sin(psi)).astype(np.float32),
    )


def prep_kernel(f_hbm, k_hbm, v_hbm, q_hbm, og_hbm, out_ref, held, sems):
    owners, three, rows = out_ref.shape
    chans = three // 3
    copies = [
        pltpu.make_async_copy(src, held.at[i], sems.at[i]) for i, src in enumerate((f_hbm, k_hbm, v_hbm, q_hbm, og_hbm))
    ]
    for copy in copies:
        copy.start()

    def put(slot, block):
        out_ref[:, slot * chans : (slot + 1) * chans, :] = block.T.reshape(owners, chans, rows)

    copies[0].wait()
    put(1, held[0])
    copies[1].wait()
    copies[2].wait()
    put(0, held[1] * held[2])
    copies[3].wait()
    copies[4].wait()
    put(2, held[3] * held[4])


def halve(me, blocks, own_ref, other_ref):
    for dz in range(4):
        for dx in range(4):
            own_ref[dz, dx] = blocks[block_of(me, dz, dx, 0)]
            other_ref[dz, dx] = blocks[block_of(me, dz, dx, 1)]


def across_kernel(own_ref, other_ref, after_ref, out_ref):
    for sc, ref in enumerate((own_ref, other_ref)):
        for near in range(2):
            for dx in range(4):
                out_ref[sc, near, dx] = ref[2 + near, dx]


STEPS = [(near, dx) for near in range(2) for dx in range(4)]


def near_kernel(own_ref, other_ref, across_ref, *outs):
    for (near, dx), out in zip(STEPS, outs):
        for sc, ref in enumerate((own_ref, other_ref)):
            out[0, sc] = ref[near, dx]
            out[1, sc] = across_ref[sc, near, dx]


def gather(me, arrived, x_ref):
    for (near, dx), ref in zip(STEPS, arrived):
        for far in range(2):
            for sc in range(2):
                x_ref[block_of(me, near ^ (2 * far), -dx, sc)] = ref[far, sc]


def dot(a, b):
    return jnp.dot(a, b, preferred_element_type=F32)


def spectrum(items, first_ref, second_ref, twr, twi, t_ref):
    chans, groups, rows = items.shape
    h = rows // 2
    for c in range(chans):
        part = dot(first_ref[...], items[c])
        real, imag = part[:groups], part[groups:]
        tr, ti = real * twr - imag * twi, real * twi + imag * twr
        lines = slice(c * groups, (c + 1) * groups)
        t_ref[0, lines, :h] = (tr[:, :h] + tr[:, h:]).astype(BF16)
        t_ref[0, lines, h:] = (ti[:, :h] + ti[:, h:]).astype(BF16)
        t_ref[1, lines, :h] = (tr[:, :h] - tr[:, h:]).astype(BF16)
        t_ref[1, lines, h:] = (ti[:, :h] - ti[:, h:]).astype(BF16)
    return [dot(t_ref[parity], second_ref[parity]) for parity in (0, 1)]


def products(left, right, h, conjugate):
    lr, li, rr, ri = left[:, :h], left[:, h:], right[:, :h], right[:, h:]
    if conjugate:
        real, imag = lr * rr + li * ri, lr * ri - li * rr
    else:
        real, imag = lr * rr - li * ri, lr * ri + li * rr
    return jnp.concatenate([real.astype(BF16), imag.astype(BF16)], axis=1)


def signal(scale, even, odd, first_t_ref, twr, twi, v_ref):
    chans, twice, rows = v_ref.shape
    groups = twice // 2
    h = rows // 2
    even, odd = even.reshape(chans, groups, rows), odd.reshape(chans, groups, rows)
    for part, lanes in ((even + odd, slice(0, h)), (even - odd, slice(h, rows))):
        real, imag = part[:, :, :h], part[:, :, h:]
        v_ref[:, :groups, lanes] = (real * twr[:, lanes] + imag * twi[:, lanes]).astype(BF16)
        v_ref[:, groups:, lanes] = (imag * twr[:, lanes] - real * twi[:, lanes]).astype(BF16)
    out = jnp.stack([dot(first_t_ref[...], v_ref[c]) * scale for c in range(chans)], axis=0)
    return jnp.swapaxes(out.astype(BF16), 0, 1)


def forward_kernel(
    scale,
    x_ref,
    first_ref,
    first_t_ref,
    second_ref,
    second_t_ref,
    twr_ref,
    twi_ref,
    own_ref,
    other_ref,
    spec_ref,
    t_ref,
    v_ref,
    y_ref,
):
    groups, three, rows = x_ref.shape
    chans = three // 3
    h = rows // 2
    twr, twi = twr_ref[...], twi_ref[...]
    for s in range(2):
        items = jnp.swapaxes(x_ref[:, s * chans : (s + 1) * chans, :], 0, 1)
        for parity, bins in enumerate(spectrum(items, first_ref, second_ref, twr, twi, t_ref.at[s])):
            spec_ref[s, parity] = bins
    even, odd = (
        dot(products(spec_ref[0, parity], spec_ref[1, parity], h, False), second_t_ref[parity]) for parity in (0, 1)
    )
    y_ref[...] = signal(scale, even, odd, first_t_ref, twr, twi, v_ref)
    halve(lax.axis_index("context"), y_ref, own_ref, other_ref)


def backward_kernel(
    scale,
    x_ref,
    spec_ref,
    first_ref,
    first_t_ref,
    second_ref,
    second_t_ref,
    twr_ref,
    twi_ref,
    y_hbm,
    t_ref,
    v_ref,
    y_ref,
    sems,
):
    groups, three, rows = x_ref.shape
    chans = three // 3
    h = rows // 2
    twr, twi = twr_ref[...], twi_ref[...]
    items = jnp.swapaxes(x_ref[:, 2 * chans :, :], 0, 1)
    delta = spectrum(items, first_ref, second_ref, twr, twi, t_ref)
    copies = []
    for s in range(2):
        even, odd = (
            dot(products(spec_ref[1 - s, parity], delta[parity], h, True), second_t_ref[parity]) for parity in (0, 1)
        )
        y_ref[s] = signal(scale, even, odd, first_t_ref, twr, twi, v_ref.at[s])
        copy = pltpu.make_async_copy(y_ref.at[s], y_hbm.at[:, pl.ds(s * chans, chans), :], sems.at[s])
        copy.start()
        copies.append(copy)
    for copy in copies:
        copy.wait()


class Writer:
    def __init__(self, outs, held, sems):
        self.outs, self.held, self.sems, self.copies = outs, held, sems, []

    def put(self, i, p, block):
        step = self.held.shape[2]
        self.held[i, p] = block.astype(BF16)
        copy = pltpu.make_async_copy(self.held.at[i, p], self.outs[i].at[pl.ds(p * step, step)], self.sems.at[i, p])
        copy.start()
        self.copies.append(copy)

    def wait(self):
        for copy in self.copies:
            copy.wait()


def forward_gate_kernel(*refs):
    arrived = refs[:8]
    q_ref, k_ref, v_ref, og_ref, bias_ref, mixed_hbm, qg_hbm, x_ref, held, sems = refs[8:]
    gather(lax.axis_index("context"), arrived, x_ref)
    owners, chans, rows = x_ref.shape
    writer = Writer((mixed_hbm, qg_hbm), held, sems)
    parts, step = held.shape[1:3]
    for p in range(parts):
        span = slice(p * step, (p + 1) * step)
        term = x_ref[:, :, span].reshape(owners * chans, step).T
        pre_gate = term.astype(F32) + bias_ref[...] * (k_ref[span] * v_ref[span]).astype(F32)
        writer.put(0, p, q_ref[span].astype(F32) * pre_gate)
        writer.put(1, p, og_ref[span].astype(F32) * pre_gate)
    writer.wait()


def backward_gate_kernel(y_ref, q_ref, k_ref, v_ref, og_ref, bias_ref, kg_hbm, vg_hbm, fg_hbm, held, sems):
    owners, pair, rows = y_ref.shape
    chans = pair // 2
    writer = Writer((kg_hbm, vg_hbm, fg_hbm), held, sems)
    parts, step = held.shape[1:3]
    for p in range(parts):
        span = slice(p * step, (p + 1) * step)

        def take(slot):
            return y_ref[:, slot * chans : (slot + 1) * chans, span].reshape(owners * chans, step).T

        writer.put(2, p, take(1))
        gated_grad = take(0).astype(F32) + bias_ref[...] * (og_ref[span] * q_ref[span]).astype(F32)
        writer.put(0, p, gated_grad * v_ref[span].astype(F32))
        writer.put(1, p, gated_grad * k_ref[span].astype(F32))
    writer.wait()


def local(q_gate, k_gate, v_input, filter_taps, skip_bias, out_grad):
    groups = lax.axis_size("context")
    rows, width = q_gate.shape
    chans = width // groups
    order = device_order(groups)
    seq = groups * rows
    scale = 2.0 / (2 * seq) / math.sqrt(seq)
    messages = jax.ShapeDtypeStruct((groups, 3 * chans, rows), BF16)
    whole = jax.ShapeDtypeStruct((rows, width), BF16)
    limit = pltpu.CompilerParams(vmem_limit_bytes=48 * 1024 * 1024)
    far = pl.BlockSpec(memory_space=pltpu.HBM)
    near = pl.BlockSpec(memory_space=pltpu.VMEM)

    def swap(block):
        return lax.all_to_all(
            block, "context", split_axis=0, concat_axis=0, tiled=True, axis_index_groups=[order]
        )

    block = (chans, rows)
    bins = (chans * groups, rows)

    def call(kernel, name, out_shape, scratch_shapes=(), weight=0, **more):
        if weight:
            more["cost_estimate"] = pl.CostEstimate(flops=weight, bytes_accessed=weight, transcendentals=0)
        return pl.pallas_call(
            kernel, out_shape=out_shape, scratch_shapes=list(scratch_shapes), compiler_params=limit, name=name, **more
        )

    def shape(*dims):
        return jax.ShapeDtypeStruct(dims, BF16)

    def travel(own, other, after):
        other = send(other, 0, 0, 1)
        across = call(
            across_kernel,
            "across",
            shape(2, 2, 4, *block),
            weight=WEIGHT,
            in_specs=[near] * 2 + [pl.BlockSpec(memory_space=pl.ANY)],
            out_specs=near,
        )(own, other, after)
        across = send(across, 2, 0, 0)
        kept, *leaving = call(near_kernel, "near", [shape(2, 2, *block)] * 8, weight=WEIGHT)(own, other, across)
        return [kept] + [send(part, dz, dx, 0) for part, (dz, dx) in zip(leaving, STEPS[1:])]

    first, first_t, second, second_t, twr, twi = make_tables(order, rows)
    sent = call(
        prep_kernel,
        "gate_and_pack",
        pltpu.VMEM(messages.shape, BF16),
        [pltpu.VMEM((5, rows, width), BF16), pltpu.SemaphoreType.DMA((5,))],
        in_specs=[far] * 5,
        out_specs=near,
    )(*(pltpu.with_memory_space_constraint(x, pltpu.HBM) for x in (filter_taps, k_gate, v_input, q_gate, out_grad)))
    items = swap(sent)
    own, other, spec = call(
        functools.partial(forward_kernel, scale),
        "forward",
        [shape(4, 4, *block)] * 2 + [jax.ShapeDtypeStruct((2, 2, *bins), F32)],
        [pltpu.VMEM((2, 2, *bins), BF16), pltpu.VMEM((chans, 2 * groups, rows), BF16), pltpu.VMEM((groups, *block), BF16)],
    )(items, first, first_t, second, second_t, twr, twi)
    terms = call(
        functools.partial(backward_kernel, scale),
        "backward",
        shape(groups, 2 * chans, rows),
        [
            pltpu.VMEM((2, *bins), BF16),
            pltpu.VMEM((2, chans, 2 * groups, rows), BF16),
            pltpu.VMEM((2, groups, *block), BF16),
            pltpu.SemaphoreType.DMA((2,)),
        ],
        in_specs=[near] * 8,
        out_specs=far,
    )(items, spec, first, first_t, second, second_t, twr, twi)
    arrived = travel(own, other, terms)
    gates = (q_gate, k_gate, v_input, out_grad, skip_bias[None, :])
    parts = 2

    def held(outs):
        return [pltpu.VMEM((outs, parts, rows // parts, width), BF16), pltpu.SemaphoreType.DMA((outs, parts))]

    mixed, q_grad = call(
        forward_gate_kernel,
        "gate_forward",
        [whole] * 2,
        [pltpu.VMEM((groups, *block), BF16)] + held(2),
        weight=WEIGHT,
        in_specs=[near] * 13,
        out_specs=[far] * 2,
    )(*arrived, *gates)
    k_grad, v_grad, filter_grad = call(
        backward_gate_kernel, "gate_backward", [whole] * 3, held(3), in_specs=[near] * 6, out_specs=[far] * 3
    )(swap(terms), *gates)
    return mixed, q_grad, k_grad, v_grad, filter_grad


def solution(mesh):
    spec = P("context", "tensor")
    return jax.shard_map(
        local,
        mesh=mesh,
        in_specs=(spec, spec, spec, spec, P("tensor"), spec),
        out_specs=(spec,) * 5,
        check_vma=False,
    )
```

```python
import functools
import math

import jax
import jax.numpy as jnp
import ml_dtypes
import numpy as np
from jax import lax
from jax.experimental import pallas as pl
from jax.experimental.pallas import tpu as pltpu
from jax.sharding import PartitionSpec as P

BF16 = jnp.bfloat16
ZORDER = (1, 2, 3)
F32 = jnp.float32
WEIGHT1 = 5 * 10**9
WEIGHT = 8 * 10**9


QUARTERS = 4


def place(here):
    along = 4
    return here // (2 * along), here // 2 % along, here % 2


def block_of(here, dz, dx, dc):
    z, x, c = place(here)
    z = z ^ dz
    return ((z ^ (1 - z // 2)) * 4 + (x + dx) % 4) * 2 + (c ^ dc)


def device_order(groups):
    return [block_of(here, 0, 0, 0) for here in range(groups)]


def send(block, dz, dx, dc):
    groups = lax.axis_size("context")
    order = device_order(groups)
    moves = [(here, order[block_of(here, dz, dx, dc)]) for here in range(groups)]
    return lax.ppermute(block, "context", moves)


def make_tables(order, rows):
    groups = len(order)
    length = 2 * groups * rows
    a = np.array(order)[None, :]
    b = np.arange(rows)[None, :]
    half = np.arange(groups)[:, None] + 0.5
    theta = 2.0 * math.pi * a * half / (2 * groups)
    first = np.concatenate([np.cos(theta), -np.sin(theta)], axis=0)
    psi = 2.0 * math.pi * b * half / length
    low = np.arange(rows // 2)[:, None]
    m = np.arange(rows // 2)[None, :]
    second = []
    for parity in (0, 1):
        phi = 2.0 * math.pi * ((low * (2 * m + parity)) % rows) / rows
        second.append(np.block([[np.cos(phi), -np.sin(phi)], [np.sin(phi), np.cos(phi)]]))
    second = np.stack(second)
    narrow = ml_dtypes.bfloat16
    return (
        first.astype(narrow),
        np.ascontiguousarray(first.T).astype(narrow),
        second.astype(narrow),
        np.ascontiguousarray(second.transpose(0, 2, 1)).astype(narrow),
        np.cos(psi).astype(np.float32),
        (-np.sin(psi)).astype(np.float32),
    )


def halve(me, blocks, own_ref, other_ref):
    for dz in range(4):
        for dx in range(4):
            own_ref[dz, dx] = blocks[block_of(me, dz, dx, 0)]
            other_ref[dz, dx] = blocks[block_of(me, dz, dx, 1)]


def turn(block, chans):
    rows, width = block.shape
    return block.T.reshape(width // chans, chans, rows)


def pack_early_kernel(f_hbm, k_hbm, v_hbm, own_ref, other_ref, rest_ref, held, turned, sems):
    owners, chans, h = rest_ref.shape
    rows = 2 * h
    copies = [pltpu.make_async_copy(src, held.at[i], sems.at[i]) for i, src in enumerate((f_hbm, k_hbm, v_hbm))]
    for copy in copies:
        copy.start()
    me = lax.axis_index("context")
    copies[0].wait()
    turned[:, :, :rows] = turn(held[0], chans)
    copies[1].wait()
    copies[2].wait()
    gated = turn(held[1] * held[2], chans)
    turned[:, :, rows:] = gated[:, :, :h]
    rest_ref[...] = gated[:, :, h:]
    halve(me, turned, own_ref, other_ref)


def pack_late_kernel(q_hbm, og_hbm, rest_ref, out_hbm, held, out_ref, sems):
    owners, chans, rows = out_ref.shape
    copies = [pltpu.make_async_copy(src, held.at[i], sems.at[i]) for i, src in enumerate((q_hbm, og_hbm))]
    leaving = [
        pltpu.make_async_copy(rest_ref, out_hbm.at[:, :, pl.ds(rows, rows // 2)], sems.at[2]),
        pltpu.make_async_copy(out_ref, out_hbm.at[:, :, pl.ds(0, rows)], sems.at[3]),
    ]
    for copy in copies:
        copy.start()
    leaving[0].start()
    for copy in copies:
        copy.wait()
    out_ref[...] = turn(held[0] * held[1], chans)
    leaving[1].start()
    for copy in leaving:
        copy.wait()


def along_z_kernel(own_ref, other_ref, after_ref, *outs):
    for dz, out in enumerate(outs, start=1):
        for sc, ref in enumerate((own_ref, other_ref)):
            for dx in range(4):
                out[sc, dx] = ref[dz, dx]


def along_x_kernel(own_ref, other_ref, *refs):
    arrived, outs = refs[:3], refs[3:]
    for dx, out in enumerate(outs):
        for sc, ref in enumerate((own_ref, other_ref)):
            out[0, sc] = ref[0, dx]
            for dz, ref in enumerate(arrived, start=1):
                out[dz, sc] = ref[sc, dx]


def gather(me, arrived, x_ref):
    for dx, ref in enumerate(arrived):
        for dz in range(4):
            for sc in range(2):
                x_ref[block_of(me, dz, -dx, sc)] = ref[dz, sc]


def dot(a, b):
    return jnp.dot(a, b, preferred_element_type=F32)


def spectrum(items, first_ref, second_ref, twr, twi, t_ref):
    chans, groups, rows = items.shape
    h = rows // 2
    for c in range(chans):
        part = dot(first_ref[...], items[c])
        real, imag = part[:groups], part[groups:]
        tr, ti = real * twr - imag * twi, real * twi + imag * twr
        lines = slice(c * groups, (c + 1) * groups)
        t_ref[0, lines, :h] = (tr[:, :h] + tr[:, h:]).astype(BF16)
        t_ref[0, lines, h:] = (ti[:, :h] + ti[:, h:]).astype(BF16)
        t_ref[1, lines, :h] = (tr[:, :h] - tr[:, h:]).astype(BF16)
        t_ref[1, lines, h:] = (ti[:, :h] - ti[:, h:]).astype(BF16)
    return [dot(t_ref[parity], second_ref[parity]) for parity in (0, 1)]


def filter_kernel(*refs):
    arrived = refs[:4]
    first_ref, second_ref, twr_ref, twi_ref, spec_ref, rest_ref, x_ref, t_ref = refs[4:]
    gather(lax.axis_index("context"), arrived, x_ref)
    rows = twr_ref.shape[1]
    items = jnp.swapaxes(x_ref[:, :, :rows], 0, 1)
    for parity, bins in enumerate(spectrum(items, first_ref, second_ref, twr_ref[...], twi_ref[...], t_ref)):
        spec_ref[parity] = bins
    rest_ref[...] = x_ref[:, :, rows:]


def products(left, right, h, conjugate):
    lr, li, rr, ri = left[:, :h], left[:, h:], right[:, :h], right[:, h:]
    if conjugate:
        real, imag = lr * rr + li * ri, lr * ri - li * rr
    else:
        real, imag = lr * rr - li * ri, lr * ri + li * rr
    return jnp.concatenate([real.astype(BF16), imag.astype(BF16)], axis=1)


def signal(scale, even, odd, first_t_ref, twr, twi, v_ref):
    chans, twice, rows = v_ref.shape
    groups = twice // 2
    h = rows // 2
    even, odd = even.reshape(chans, groups, rows), odd.reshape(chans, groups, rows)
    for part, lanes in ((even + odd, slice(0, h)), (even - odd, slice(h, rows))):
        real, imag = part[:, :, :h], part[:, :, h:]
        v_ref[:, :groups, lanes] = (real * twr[:, lanes] + imag * twi[:, lanes]).astype(BF16)
        v_ref[:, groups:, lanes] = (imag * twr[:, lanes] - real * twi[:, lanes]).astype(BF16)
    out = jnp.stack([dot(first_t_ref[...], v_ref[c]) * scale for c in range(chans)], axis=0)
    return jnp.swapaxes(out.astype(BF16), 0, 1)


def forward_kernel(
    scale,
    x_ref,
    taps_ref,
    part_ref,
    first_ref,
    first_t_ref,
    second_ref,
    second_t_ref,
    twr_ref,
    twi_ref,
    own_ref,
    other_ref,
    rest_ref,
    spec_ref,
    t_ref,
    v_ref,
    y_ref,
):
    rows = twr_ref.shape[1]
    h = rows // 2
    twr, twi = twr_ref[...], twi_ref[...]
    gated = jnp.concatenate([part_ref[...], x_ref[:, :, rows:]], axis=2)
    spectra = [
        spectrum(jnp.swapaxes(block, 0, 1), first_ref, second_ref, twr, twi, t_ref.at[s])
        for s, block in enumerate((gated, x_ref[:, :, :rows]))
    ]
    gated, delta = spectra
    taps = taps_ref
    for parity in (0, 1):
        spec_ref[0, parity] = gated[parity]
        spec_ref[1, parity] = delta[parity]
    even, odd = (dot(products(gated[parity], taps[parity], h, False), second_t_ref[parity]) for parity in (0, 1))
    y_ref[:, :, :rows] = signal(scale, even, odd, first_t_ref, twr, twi, v_ref.at[0])
    even, odd = (dot(products(taps[parity], delta[parity], h, True), second_t_ref[parity]) for parity in (0, 1))
    back = signal(scale, even, odd, first_t_ref, twr, twi, v_ref.at[1])
    y_ref[:, :, rows:] = back[:, :, :h]
    rest_ref[...] = back[:, :, h:]
    halve(lax.axis_index("context"), y_ref, own_ref, other_ref)


def backward_kernel(
    scale, spec_ref, rest_ref, first_t_ref, second_t_ref, twr_ref, twi_ref, y_hbm, v_ref, y_ref, sems
):
    groups, chans, rows = y_ref.shape
    h = rows // 2
    twr, twi = twr_ref[...], twi_ref[...]
    copies = [
        pltpu.make_async_copy(rest_ref, y_hbm.at[:, :, pl.ds(rows, h)], sems.at[0]),
        pltpu.make_async_copy(y_ref, y_hbm.at[:, :, pl.ds(0, rows)], sems.at[1]),
    ]
    copies[0].start()
    even, odd = (dot(products(spec_ref[0, parity], spec_ref[1, parity], h, True), second_t_ref[parity]) for parity in (0, 1))
    y_ref[...] = signal(scale, even, odd, first_t_ref, twr, twi, v_ref)
    copies[1].start()
    for copy in copies:
        copy.wait()


class Writer:
    def __init__(self, outs, held, sems):
        self.outs, self.held, self.sems, self.copies = outs, held, sems, []

    def put(self, i, p, block):
        step = self.held.shape[2]
        self.held[i, p] = block.astype(BF16)
        copy = pltpu.make_async_copy(self.held.at[i, p], self.outs[i].at[pl.ds(p * step, step)], self.sems.at[i, p])
        copy.start()
        self.copies.append(copy)

    def wait(self):
        for copy in self.copies:
            copy.wait()


def gate_kernel(*refs):
    arrived = refs[:4]
    y_ref, q_ref, k_ref, v_ref, og_ref, bias_ref, mixed_hbm, qg_hbm, kg_hbm, vg_hbm, fg_hbm, x_ref, held, sems = refs[4:]
    owners, chans, _ = x_ref.shape
    writer = Writer((mixed_hbm, qg_hbm, kg_hbm, vg_hbm, fg_hbm), held, sems)
    parts, step = held.shape[1:3]
    bias = bias_ref[...]

    def take(ref, p):
        return ref[:, :, p * step : (p + 1) * step].reshape(owners * chans, step).T

    for p in range(parts):
        writer.put(4, p, take(y_ref, p))
    gather(lax.axis_index("context"), arrived, x_ref)
    for p in range(parts):
        span = slice(p * step, (p + 1) * step)
        q, k, v, og = q_ref[span], k_ref[span], v_ref[span], og_ref[span]
        pre_gate = take(x_ref, p).astype(F32) + bias * (k * v).astype(F32)
        writer.put(0, p, q.astype(F32) * pre_gate)
        writer.put(1, p, og.astype(F32) * pre_gate)
        back = take((x_ref, y_ref)[p], parts)
        gated_grad = back.astype(F32) + bias * (og * q).astype(F32)
        writer.put(2, p, gated_grad * v.astype(F32))
        writer.put(3, p, gated_grad * k.astype(F32))
    writer.wait()


def local(q_gate, k_gate, v_input, filter_taps, skip_bias, out_grad):
    groups = lax.axis_size("context")
    rows, width = q_gate.shape
    chans = width // groups
    order = device_order(groups)
    seq = groups * rows
    scale = 2.0 / (2 * seq) / math.sqrt(seq)
    messages = jax.ShapeDtypeStruct((groups, 3 * chans, rows), BF16)
    whole = jax.ShapeDtypeStruct((rows, width), BF16)
    limit = pltpu.CompilerParams(vmem_limit_bytes=48 * 1024 * 1024)
    far = pl.BlockSpec(memory_space=pltpu.HBM)
    near = pl.BlockSpec(memory_space=pltpu.VMEM)

    def swap(block):
        return lax.all_to_all(
            block, "context", split_axis=0, concat_axis=0, tiled=True, axis_index_groups=[order]
        )

    block = (chans, rows + rows // 2)
    bins = (chans * groups, rows)

    def call(kernel, name, out_shape, scratch_shapes=(), weight=0, **more):
        if weight:
            more["cost_estimate"] = pl.CostEstimate(flops=weight, bytes_accessed=weight, transcendentals=0)
        return pl.pallas_call(
            kernel, out_shape=out_shape, scratch_shapes=list(scratch_shapes), compiler_params=limit, name=name, **more
        )

    def shape(*dims):
        return jax.ShapeDtypeStruct(dims, BF16)

    def travel(own, other, after, weight):
        other = send(other, 0, 0, 1)
        leaving = call(
            along_z_kernel,
            "along_z",
            [shape(2, 4, *own.shape[2:])] * 3,
            weight=weight,
            in_specs=[near] * 2 + [pl.BlockSpec(memory_space=pl.ANY)],
            out_specs=[near] * 3,
        )(own, other, after)
        arrived = [None] * 3
        for dz in ZORDER:
            arrived[dz - 1] = send(leaving[dz - 1], dz, 0, 0)
        kept, *leaving = call(along_x_kernel, "along_x", [shape(4, 2, *own.shape[2:])] * 4, weight=weight)(
            own, other, *arrived
        )
        return [kept] + [send(part, 0, dx, 0) for dx, part in enumerate(leaving, start=1)]

    first, first_t, second, second_t, twr, twi = make_tables(order, rows)
    def keep(*arrays):
        return [pltpu.with_memory_space_constraint(x, pltpu.HBM) for x in arrays]

    one, half = (chans, rows), (chans, rows // 2)
    own, other, rest = call(
        pack_early_kernel,
        "pack_early",
        [pltpu.VMEM((4, 4, *block), BF16)] * 2 + [pltpu.VMEM((groups, *half), BF16)],
        [pltpu.VMEM((3, rows, width), BF16), pltpu.VMEM((groups, *block), BF16), pltpu.SemaphoreType.DMA((3,))],
        in_specs=[far] * 3,
        out_specs=[near] * 3,
    )(*keep(filter_taps, k_gate, v_input))
    sent = call(
        pack_late_kernel,
        "pack_late",
        shape(groups, *block),
        [pltpu.VMEM((2, rows, width), BF16), pltpu.VMEM((groups, *one), BF16), pltpu.SemaphoreType.DMA((4,))],
        in_specs=[far] * 2 + [near],
        out_specs=far,
    )(*keep(q_gate, out_grad), rest)
    taps, part = call(
        filter_kernel,
        "filter_spectrum",
        [jax.ShapeDtypeStruct((2, *bins), F32), shape(groups, *half)],
        [pltpu.VMEM((groups, *block), BF16), pltpu.VMEM((2, *bins), BF16)],
        weight=WEIGHT1,
    )(*travel(own, other, sent, WEIGHT1), first, second, twr, twi)
    items = swap(sent)
    own, other, rest, spec = call(
        functools.partial(forward_kernel, scale),
        "forward",
        [shape(4, 4, *block)] * 2
        + [shape(groups, *half), jax.ShapeDtypeStruct((2, 2, *bins), F32)],
        [
            pltpu.VMEM((2, 2, *bins), BF16),
            pltpu.VMEM((2, chans, 2 * groups, rows), BF16),
            pltpu.VMEM((groups, *block), BF16),
        ],
    )(items, taps, part, first, first_t, second, second_t, twr, twi)
    terms = call(
        functools.partial(backward_kernel, scale),
        "backward",
        shape(groups, *block),
        [
            pltpu.VMEM((chans, 2 * groups, rows), BF16),
            pltpu.VMEM((groups, *one), BF16),
            pltpu.SemaphoreType.DMA((2,)),
        ],
        in_specs=[near] * 6,
        out_specs=far,
    )(spec, rest, first_t, second_t, twr, twi)
    arrived = travel(own, other, terms, WEIGHT)
    parts = 2
    return call(
        gate_kernel,
        "gate",
        [whole] * 5,
        [
            pltpu.VMEM((groups, *block), BF16),
            pltpu.VMEM((5, parts, rows // parts, width), BF16),
            pltpu.SemaphoreType.DMA((5, parts)),
        ],
        in_specs=[near] * 10,
        out_specs=[far] * 5,
    )(*arrived, swap(terms), q_gate, k_gate, v_input, out_grad, skip_bias[None, :])


def solution(mesh):
    spec = P("context", "tensor")
    return jax.shard_map(
        local,
        mesh=mesh,
        in_specs=(spec, spec, spec, spec, P("tensor"), spec),
        out_specs=(spec,) * 5,
        check_vma=False,
    )
```

```python
import functools
import math

import jax
import jax.numpy as jnp
import ml_dtypes
import numpy as np
from jax import lax
from jax.experimental import pallas as pl
from jax.experimental.pallas import tpu as pltpu
from jax.sharding import PartitionSpec as P

BF16 = jnp.bfloat16
ZORDER = (1, 2, 3)
F32 = jnp.float32
WEIGHT1 = 5 * 10**9
WEIGHT = 8 * 10**9


QUARTERS = 4


def place(here):
    along = 4
    return here // (2 * along), here // 2 % along, here % 2


def block_of(here, dz, dx, dc):
    z, x, c = place(here)
    z = z ^ dz
    return (((x + dx) % 4) * 2 + (c ^ dc)) * 4 + (z ^ (1 - z // 2))


def device_order(groups):
    return sorted(range(groups), key=lambda here: block_of(here, 0, 0, 0))


def send(block, dz, dx, dc):
    groups = lax.axis_size("context")
    order = device_order(groups)
    moves = [(here, order[block_of(here, dz, dx, dc)]) for here in range(groups)]
    return lax.ppermute(block, "context", moves)


def make_tables(order, rows):
    groups = len(order)
    length = 2 * groups * rows
    a = np.array(order)[None, :]
    b = np.arange(rows)[None, :]
    half = np.arange(groups)[:, None] + 0.5
    theta = 2.0 * math.pi * a * half / (2 * groups)
    first = np.concatenate([np.cos(theta), -np.sin(theta)], axis=0)
    psi = 2.0 * math.pi * b * half / length
    low = np.arange(rows // 2)[:, None]
    m = np.arange(rows // 2)[None, :]
    second = []
    for parity in (0, 1):
        phi = 2.0 * math.pi * ((low * (2 * m + parity)) % rows) / rows
        second.append(np.block([[np.cos(phi), -np.sin(phi)], [np.sin(phi), np.cos(phi)]]))
    second = np.stack(second)
    narrow = ml_dtypes.bfloat16
    return (
        first.astype(narrow),
        np.ascontiguousarray(first.T).astype(narrow),
        second.astype(narrow),
        np.ascontiguousarray(second.transpose(0, 2, 1)).astype(narrow),
        np.cos(psi).astype(np.float32),
        (-np.sin(psi)).astype(np.float32),
    )


def halve(me, blocks, own_ref, other_ref):
    for dz in range(4):
        for dx in range(4):
            own_ref[dz, dx] = blocks[block_of(me, dz, dx, 0)]
            other_ref[dz, dx] = blocks[block_of(me, dz, dx, 1)]


def turn(block, chans):
    rows, width = block.shape
    return block.T.reshape(width // chans, chans, rows)


def pack_early_kernel(f_hbm, k_hbm, v_hbm, own_ref, other_ref, rest_ref, held, turned, sems):
    owners, chans, h = rest_ref.shape
    rows = 2 * h
    copies = [pltpu.make_async_copy(src, held.at[i], sems.at[i]) for i, src in enumerate((f_hbm, k_hbm, v_hbm))]
    for copy in copies:
        copy.start()
    me = lax.axis_index("context")
    copies[0].wait()
    turned[:, :, :rows] = turn(held[0], chans)
    copies[1].wait()
    copies[2].wait()
    gated = turn(held[1] * held[2], chans)
    turned[:, :, rows:] = gated[:, :, :h]
    rest_ref[...] = gated[:, :, h:]
    halve(me, turned, own_ref, other_ref)


def pack_late_kernel(q_hbm, og_hbm, rest_ref, out_hbm, held, out_ref, sems):
    owners, chans, rows = out_ref.shape
    copies = [pltpu.make_async_copy(src, held.at[i], sems.at[i]) for i, src in enumerate((q_hbm, og_hbm))]
    leaving = [
        pltpu.make_async_copy(rest_ref, out_hbm.at[:, :, pl.ds(rows, rows // 2)], sems.at[2]),
        pltpu.make_async_copy(out_ref, out_hbm.at[:, :, pl.ds(0, rows)], sems.at[3]),
    ]
    for copy in copies:
        copy.start()
    leaving[0].start()
    for copy in copies:
        copy.wait()
    out_ref[...] = turn(held[0] * held[1], chans)
    leaving[1].start()
    for copy in leaving:
        copy.wait()


def along_z_kernel(own_ref, other_ref, after_ref, *outs):
    for dz, out in enumerate(outs, start=1):
        for sc, ref in enumerate((own_ref, other_ref)):
            for dx in range(4):
                out[sc, dx] = ref[dz, dx]


def along_x_kernel(own_ref, other_ref, *refs):
    arrived, outs = refs[:3], refs[3:]
    for dx, out in enumerate(outs):
        for sc, ref in enumerate((own_ref, other_ref)):
            out[0, sc] = ref[0, dx]
            for dz, ref in enumerate(arrived, start=1):
                out[dz, sc] = ref[sc, dx]


def gather(me, arrived, x_ref):
    for dx, ref in enumerate(arrived):
        for dz in range(4):
            for sc in range(2):
                x_ref[block_of(me, dz, -dx, sc)] = ref[dz, sc]


def dot(a, b):
    return jnp.dot(a, b, preferred_element_type=F32)


def spectrum(items, first_ref, second_ref, twr, twi, t_ref):
    chans, groups, rows = items.shape
    h = rows // 2
    for c in range(chans):
        part = dot(first_ref[...], items[c])
        real, imag = part[:groups], part[groups:]
        tr, ti = real * twr - imag * twi, real * twi + imag * twr
        lines = slice(c * groups, (c + 1) * groups)
        t_ref[0, lines, :h] = (tr[:, :h] + tr[:, h:]).astype(BF16)
        t_ref[0, lines, h:] = (ti[:, :h] + ti[:, h:]).astype(BF16)
        t_ref[1, lines, :h] = (tr[:, :h] - tr[:, h:]).astype(BF16)
        t_ref[1, lines, h:] = (ti[:, :h] - ti[:, h:]).astype(BF16)
    return [dot(t_ref[parity], second_ref[parity]) for parity in (0, 1)]


def filter_kernel(*refs):
    arrived = refs[:4]
    first_ref, second_ref, twr_ref, twi_ref, spec_ref, rest_ref, x_ref, t_ref = refs[4:]
    gather(lax.axis_index("context"), arrived, x_ref)
    rows = twr_ref.shape[1]
    items = jnp.swapaxes(x_ref[:, :, :rows], 0, 1)
    for parity, bins in enumerate(spectrum(items, first_ref, second_ref, twr_ref[...], twi_ref[...], t_ref)):
        spec_ref[parity] = bins
    rest_ref[...] = x_ref[:, :, rows:]


def products(left, right, h, conjugate):
    lr, li, rr, ri = left[:, :h], left[:, h:], right[:, :h], right[:, h:]
    if conjugate:
        real, imag = lr * rr + li * ri, lr * ri - li * rr
    else:
        real, imag = lr * rr - li * ri, lr * ri + li * rr
    return jnp.concatenate([real.astype(BF16), imag.astype(BF16)], axis=1)


def signal(scale, even, odd, first_t_ref, twr, twi, v_ref):
    chans, twice, rows = v_ref.shape
    groups = twice // 2
    h = rows // 2
    even, odd = even.reshape(chans, groups, rows), odd.reshape(chans, groups, rows)
    for part, lanes in ((even + odd, slice(0, h)), (even - odd, slice(h, rows))):
        real, imag = part[:, :, :h], part[:, :, h:]
        v_ref[:, :groups, lanes] = (real * twr[:, lanes] + imag * twi[:, lanes]).astype(BF16)
        v_ref[:, groups:, lanes] = (imag * twr[:, lanes] - real * twi[:, lanes]).astype(BF16)
    out = jnp.stack([dot(first_t_ref[...], v_ref[c]) * scale for c in range(chans)], axis=0)
    return jnp.swapaxes(out.astype(BF16), 0, 1)


def forward_kernel(
    scale,
    x_ref,
    taps_ref,
    part_ref,
    first_ref,
    first_t_ref,
    second_ref,
    second_t_ref,
    twr_ref,
    twi_ref,
    own_ref,
    other_ref,
    rest_ref,
    spec_ref,
    t_ref,
    v_ref,
    y_ref,
):
    rows = twr_ref.shape[1]
    h = rows // 2
    twr, twi = twr_ref[...], twi_ref[...]
    gated = jnp.concatenate([part_ref[...], x_ref[:, :, rows:]], axis=2)
    spectra = [
        spectrum(jnp.swapaxes(block, 0, 1), first_ref, second_ref, twr, twi, t_ref.at[s])
        for s, block in enumerate((gated, x_ref[:, :, :rows]))
    ]
    gated, delta = spectra
    taps = taps_ref
    for parity in (0, 1):
        spec_ref[0, parity] = gated[parity]
        spec_ref[1, parity] = delta[parity]
    even, odd = (dot(products(gated[parity], taps[parity], h, False), second_t_ref[parity]) for parity in (0, 1))
    y_ref[:, :, :rows] = signal(scale, even, odd, first_t_ref, twr, twi, v_ref.at[0])
    even, odd = (dot(products(taps[parity], delta[parity], h, True), second_t_ref[parity]) for parity in (0, 1))
    back = signal(scale, even, odd, first_t_ref, twr, twi, v_ref.at[1])
    y_ref[:, :, rows:] = back[:, :, :h]
    rest_ref[...] = back[:, :, h:]
    halve(lax.axis_index("context"), y_ref, own_ref, other_ref)


def backward_kernel(
    scale, spec_ref, rest_ref, first_t_ref, second_t_ref, twr_ref, twi_ref, y_hbm, v_ref, y_ref, sems
):
    groups, chans, rows = y_ref.shape
    h = rows // 2
    twr, twi = twr_ref[...], twi_ref[...]
    copies = [
        pltpu.make_async_copy(rest_ref, y_hbm.at[:, :, pl.ds(rows, h)], sems.at[0]),
        pltpu.make_async_copy(y_ref, y_hbm.at[:, :, pl.ds(0, rows)], sems.at[1]),
    ]
    copies[0].start()
    even, odd = (dot(products(spec_ref[0, parity], spec_ref[1, parity], h, True), second_t_ref[parity]) for parity in (0, 1))
    y_ref[...] = signal(scale, even, odd, first_t_ref, twr, twi, v_ref)
    copies[1].start()
    for copy in copies:
        copy.wait()


class Writer:
    def __init__(self, outs, held, sems):
        self.outs, self.held, self.sems, self.copies = outs, held, sems, []

    def put(self, i, p, block):
        step = self.held.shape[2]
        self.held[i, p] = block.astype(BF16)
        copy = pltpu.make_async_copy(self.held.at[i, p], self.outs[i].at[pl.ds(p * step, step)], self.sems.at[i, p])
        copy.start()
        self.copies.append(copy)

    def wait(self):
        for copy in self.copies:
            copy.wait()


def gate_kernel(*refs):
    arrived = refs[:4]
    y_ref, q_ref, k_ref, v_ref, og_ref, bias_ref, mixed_hbm, qg_hbm, kg_hbm, vg_hbm, fg_hbm, x_ref, held, sems = refs[4:]
    owners, chans, _ = x_ref.shape
    writer = Writer((mixed_hbm, qg_hbm, kg_hbm, vg_hbm, fg_hbm), held, sems)
    parts, step = held.shape[1:3]
    bias = bias_ref[...]

    def take(ref, p):
        return ref[:, :, p * step : (p + 1) * step].reshape(owners * chans, step).T

    for p in range(parts):
        writer.put(4, p, take(y_ref, p))
    gather(lax.axis_index("context"), arrived, x_ref)
    for p in range(parts):
        span = slice(p * step, (p + 1) * step)
        q, k, v, og = q_ref[span], k_ref[span], v_ref[span], og_ref[span]
        pre_gate = take(x_ref, p).astype(F32) + bias * (k * v).astype(F32)
        writer.put(0, p, q.astype(F32) * pre_gate)
        writer.put(1, p, og.astype(F32) * pre_gate)
        back = take((x_ref, y_ref)[p], parts)
        gated_grad = back.astype(F32) + bias * (og * q).astype(F32)
        writer.put(2, p, gated_grad * v.astype(F32))
        writer.put(3, p, gated_grad * k.astype(F32))
    writer.wait()


def local(q_gate, k_gate, v_input, filter_taps, skip_bias, out_grad):
    groups = lax.axis_size("context")
    rows, width = q_gate.shape
    chans = width // groups
    order = device_order(groups)
    seq = groups * rows
    scale = 2.0 / (2 * seq) / math.sqrt(seq)
    messages = jax.ShapeDtypeStruct((groups, 3 * chans, rows), BF16)
    whole = jax.ShapeDtypeStruct((rows, width), BF16)
    limit = pltpu.CompilerParams(vmem_limit_bytes=48 * 1024 * 1024)
    far = pl.BlockSpec(memory_space=pltpu.HBM)
    near = pl.BlockSpec(memory_space=pltpu.VMEM)

    def swap(block):
        return lax.all_to_all(
            block, "context", split_axis=0, concat_axis=0, tiled=True, axis_index_groups=[order]
        )

    block = (chans, rows + rows // 2)
    bins = (chans * groups, rows)

    def call(kernel, name, out_shape, scratch_shapes=(), weight=0, **more):
        if weight:
            more["cost_estimate"] = pl.CostEstimate(flops=weight, bytes_accessed=weight, transcendentals=0)
        return pl.pallas_call(
            kernel, out_shape=out_shape, scratch_shapes=list(scratch_shapes), compiler_params=limit, name=name, **more
        )

    def shape(*dims):
        return jax.ShapeDtypeStruct(dims, BF16)

    def travel(own, other, after, weight):
        other = send(other, 0, 0, 1)
        leaving = call(
            along_z_kernel,
            "along_z",
            [shape(2, 4, *own.shape[2:])] * 3,
            weight=weight,
            in_specs=[near] * 2 + [pl.BlockSpec(memory_space=pl.ANY)],
            out_specs=[near] * 3,
        )(own, other, after)
        arrived = [None] * 3
        for dz in ZORDER:
            arrived[dz - 1] = send(leaving[dz - 1], dz, 0, 0)
        kept, *leaving = call(along_x_kernel, "along_x", [shape(4, 2, *own.shape[2:])] * 4, weight=weight)(
            own, other, *arrived
        )
        return [kept] + [send(part, 0, dx, 0) for dx, part in enumerate(leaving, start=1)]

    first, first_t, second, second_t, twr, twi = make_tables(order, rows)
    def keep(*arrays):
        return [pltpu.with_memory_space_constraint(x, pltpu.HBM) for x in arrays]

    one, half = (chans, rows), (chans, rows // 2)
    own, other, rest = call(
        pack_early_kernel,
        "pack_early",
        [pltpu.VMEM((4, 4, *block), BF16)] * 2 + [pltpu.VMEM((groups, *half), BF16)],
        [pltpu.VMEM((3, rows, width), BF16), pltpu.VMEM((groups, *block), BF16), pltpu.SemaphoreType.DMA((3,))],
        in_specs=[far] * 3,
        out_specs=[near] * 3,
    )(*keep(filter_taps, k_gate, v_input))
    sent = call(
        pack_late_kernel,
        "pack_late",
        shape(groups, *block),
        [pltpu.VMEM((2, rows, width), BF16), pltpu.VMEM((groups, *one), BF16), pltpu.SemaphoreType.DMA((4,))],
        in_specs=[far] * 2 + [near],
        out_specs=far,
    )(*keep(q_gate, out_grad), rest)
    taps, part = call(
        filter_kernel,
        "filter_spectrum",
        [jax.ShapeDtypeStruct((2, *bins), F32), shape(groups, *half)],
        [pltpu.VMEM((groups, *block), BF16), pltpu.VMEM((2, *bins), BF16)],
        weight=WEIGHT1,
    )(*travel(own, other, sent, WEIGHT1), first, second, twr, twi)
    items = swap(sent)
    own, other, rest, spec = call(
        functools.partial(forward_kernel, scale),
        "forward",
        [shape(4, 4, *block)] * 2
        + [shape(groups, *half), jax.ShapeDtypeStruct((2, 2, *bins), F32)],
        [
            pltpu.VMEM((2, 2, *bins), BF16),
            pltpu.VMEM((2, chans, 2 * groups, rows), BF16),
            pltpu.VMEM((groups, *block), BF16),
        ],
    )(items, taps, part, first, first_t, second, second_t, twr, twi)
    terms = call(
        functools.partial(backward_kernel, scale),
        "backward",
        shape(groups, *block),
        [
            pltpu.VMEM((chans, 2 * groups, rows), BF16),
            pltpu.VMEM((groups, *one), BF16),
            pltpu.SemaphoreType.DMA((2,)),
        ],
        in_specs=[near] * 6,
        out_specs=far,
    )(spec, rest, first_t, second_t, twr, twi)
    arrived = travel(own, other, terms, WEIGHT)
    parts = 2
    return call(
        gate_kernel,
        "gate",
        [whole] * 5,
        [
            pltpu.VMEM((groups, *block), BF16),
            pltpu.VMEM((5, parts, rows // parts, width), BF16),
            pltpu.SemaphoreType.DMA((5, parts)),
        ],
        in_specs=[near] * 10,
        out_specs=[far] * 5,
    )(*arrived, swap(terms), q_gate, k_gate, v_input, out_grad, skip_bias[None, :])


def solution(mesh):
    spec = P("context", "tensor")
    return jax.shard_map(
        local,
        mesh=mesh,
        in_specs=(spec, spec, spec, spec, P("tensor"), spec),
        out_specs=(spec,) * 5,
        check_vma=False,
    )
```

```python
import functools
import math

import jax
import jax.numpy as jnp
import ml_dtypes
import numpy as np
from jax import lax
from jax.experimental import pallas as pl
from jax.experimental.pallas import tpu as pltpu
from jax.sharding import PartitionSpec as P

BF16 = jnp.bfloat16
ZORDER = (1, 2, 3)
F32 = jnp.float32
WEIGHT1 = 5 * 10**9
WEIGHT = 8 * 10**9


QUARTERS = 4


def place(here):
    along = 4
    return here // (2 * along), here // 2 % along, here % 2


def block_of(here, dz, dx, dc):
    z, x, c = place(here)
    z = z ^ dz
    return (((x + dx) % 4) * 2 + (c ^ dc)) * 4 + (z ^ (1 - z // 2))


def device_order(groups):
    return sorted(range(groups), key=lambda here: block_of(here, 0, 0, 0))


def send(block, dz, dx, dc):
    groups = lax.axis_size("context")
    order = device_order(groups)
    moves = [(here, order[block_of(here, dz, dx, dc)]) for here in range(groups)]
    return lax.ppermute(block, "context", moves)


def make_tables(order, rows):
    groups = len(order)
    length = 2 * groups * rows
    a = np.array(order)[None, :]
    b = np.arange(rows)[None, :]
    half = np.arange(groups)[:, None] + 0.5
    theta = 2.0 * math.pi * a * half / (2 * groups)
    first = np.concatenate([np.cos(theta), -np.sin(theta)], axis=0)
    psi = 2.0 * math.pi * b * half / length
    low = np.arange(rows // 2)[:, None]
    m = np.arange(rows // 2)[None, :]
    second = []
    for parity in (0, 1):
        phi = 2.0 * math.pi * ((low * (2 * m + parity)) % rows) / rows
        second.append(np.block([[np.cos(phi), -np.sin(phi)], [np.sin(phi), np.cos(phi)]]))
    second = np.stack(second)
    narrow = ml_dtypes.bfloat16
    return (
        first.astype(narrow),
        np.ascontiguousarray(first.T).astype(narrow),
        np.stack([second, second.transpose(0, 2, 1)]).astype(narrow),
        np.cos(psi).astype(np.float32),
        (-np.sin(psi)).astype(np.float32),
    )


def halve(me, blocks, own_ref, other_ref):
    for dz in range(4):
        for dx in range(4):
            own_ref[dz, dx] = blocks[block_of(me, dz, dx, 0)]
            other_ref[dz, dx] = blocks[block_of(me, dz, dx, 1)]


def turn(block, chans):
    rows, width = block.shape
    return block.T.reshape(width // chans, chans, rows)


def pack_early_kernel(f_hbm, k_hbm, v_hbm, own_ref, other_ref, rest_ref, held, turned, sems):
    owners, chans, h = rest_ref.shape
    rows = 2 * h
    copies = [pltpu.make_async_copy(src, held.at[i], sems.at[i]) for i, src in enumerate((f_hbm, k_hbm, v_hbm))]
    for copy in copies:
        copy.start()
    me = lax.axis_index("context")
    copies[0].wait()
    turned[:, :, :rows] = turn(held[0], chans)
    copies[1].wait()
    copies[2].wait()
    gated = turn(held[1] * held[2], chans)
    turned[:, :, rows:] = gated[:, :, :h]
    rest_ref[...] = gated[:, :, h:]
    halve(me, turned, own_ref, other_ref)


def pack_late_kernel(q_hbm, og_hbm, rest_ref, out_hbm, held, out_ref, sems):
    owners, chans, rows = out_ref.shape
    copies = [pltpu.make_async_copy(src, held.at[i], sems.at[i]) for i, src in enumerate((q_hbm, og_hbm))]
    leaving = [
        pltpu.make_async_copy(rest_ref, out_hbm.at[:, :, pl.ds(rows, rows // 2)], sems.at[2]),
        pltpu.make_async_copy(out_ref, out_hbm.at[:, :, pl.ds(0, rows)], sems.at[3]),
    ]
    for copy in copies:
        copy.start()
    leaving[0].start()
    for copy in copies:
        copy.wait()
    out_ref[...] = turn(held[0] * held[1], chans)
    leaving[1].start()
    for copy in leaving:
        copy.wait()


def along_z_kernel(own_ref, other_ref, after_ref, *outs):
    for dz, out in enumerate(outs, start=1):
        for sc, ref in enumerate((own_ref, other_ref)):
            for dx in range(4):
                out[sc, dx] = ref[dz, dx]


def along_x_kernel(own_ref, other_ref, *refs):
    arrived, outs = refs[:3], refs[3:]
    for dx, out in enumerate(outs):
        for sc, ref in enumerate((own_ref, other_ref)):
            out[0, sc] = ref[0, dx]
            for dz, ref in enumerate(arrived, start=1):
                out[dz, sc] = ref[sc, dx]


def gather(me, arrived, x_ref):
    for dx, ref in enumerate(arrived):
        for dz in range(4):
            for sc in range(2):
                x_ref[block_of(me, dz, -dx, sc)] = ref[dz, sc]


def dot(a, b):
    return jnp.dot(a, b, preferred_element_type=F32)


def spectrum(items, first_ref, second_ref, twr, twi, t_ref):
    chans, groups, rows = items.shape
    h = rows // 2
    for c in range(chans):
        part = dot(first_ref[...], items[c])
        real, imag = part[:groups], part[groups:]
        tr, ti = real * twr - imag * twi, real * twi + imag * twr
        lines = slice(c * groups, (c + 1) * groups)
        t_ref[0, lines, :h] = (tr[:, :h] + tr[:, h:]).astype(BF16)
        t_ref[0, lines, h:] = (ti[:, :h] + ti[:, h:]).astype(BF16)
        t_ref[1, lines, :h] = (tr[:, :h] - tr[:, h:]).astype(BF16)
        t_ref[1, lines, h:] = (ti[:, :h] - ti[:, h:]).astype(BF16)
    return [dot(t_ref[parity], second_ref[0, parity]) for parity in (0, 1)]


def filter_kernel(*refs):
    arrived = refs[:4]
    first_ref, second_ref, twr_ref, twi_ref, spec_ref, rest_ref, x_ref, t_ref = refs[4:]
    gather(lax.axis_index("context"), arrived, x_ref)
    rows = twr_ref.shape[1]
    items = jnp.swapaxes(x_ref[:, :, :rows], 0, 1)
    for parity, bins in enumerate(spectrum(items, first_ref, second_ref, twr_ref[...], twi_ref[...], t_ref)):
        spec_ref[parity] = bins
    rest_ref[...] = x_ref[:, :, rows:]


def products(left, right, h, conjugate):
    lr, li, rr, ri = left[:, :h], left[:, h:], right[:, :h], right[:, h:]
    if conjugate:
        real, imag = lr * rr + li * ri, lr * ri - li * rr
    else:
        real, imag = lr * rr - li * ri, lr * ri + li * rr
    return jnp.concatenate([real.astype(BF16), imag.astype(BF16)], axis=1)


def signal(scale, even, odd, first_t_ref, twr, twi, v_ref):
    chans, twice, rows = v_ref.shape
    groups = twice // 2
    h = rows // 2
    even, odd = even.reshape(chans, groups, rows), odd.reshape(chans, groups, rows)
    for part, lanes in ((even + odd, slice(0, h)), (even - odd, slice(h, rows))):
        real, imag = part[:, :, :h], part[:, :, h:]
        v_ref[:, :groups, lanes] = (real * twr[:, lanes] + imag * twi[:, lanes]).astype(BF16)
        v_ref[:, groups:, lanes] = (imag * twr[:, lanes] - real * twi[:, lanes]).astype(BF16)
    out = jnp.stack([dot(first_t_ref[...], v_ref[c]) * scale for c in range(chans)], axis=0)
    return jnp.swapaxes(out.astype(BF16), 0, 1)


def forward_kernel(
    scale,
    x_ref,
    taps_ref,
    part_ref,
    first_ref,
    first_t_ref,
    second_ref,
    twr_ref,
    twi_ref,
    own_ref,
    other_ref,
    rest_ref,
    spec_ref,
    t_ref,
    v_ref,
    y_ref,
):
    rows = twr_ref.shape[1]
    h = rows // 2
    twr, twi = twr_ref[...], twi_ref[...]
    gated = jnp.concatenate([part_ref[...], x_ref[:, :, rows:]], axis=2)
    spectra = [
        spectrum(jnp.swapaxes(block, 0, 1), first_ref, second_ref, twr, twi, t_ref.at[s])
        for s, block in enumerate((gated, x_ref[:, :, :rows]))
    ]
    gated, delta = spectra
    taps = taps_ref
    for parity in (0, 1):
        spec_ref[0, parity] = gated[parity]
        spec_ref[1, parity] = delta[parity]
    even, odd = (dot(products(gated[parity], taps[parity], h, False), second_ref[1, parity]) for parity in (0, 1))
    y_ref[:, :, :rows] = signal(scale, even, odd, first_t_ref, twr, twi, v_ref.at[0])
    even, odd = (dot(products(taps[parity], delta[parity], h, True), second_ref[1, parity]) for parity in (0, 1))
    back = signal(scale, even, odd, first_t_ref, twr, twi, v_ref.at[1])
    y_ref[:, :, rows:] = back[:, :, :h]
    rest_ref[...] = back[:, :, h:]
    halve(lax.axis_index("context"), y_ref, own_ref, other_ref)


def backward_kernel(
    scale, spec_ref, rest_ref, first_t_ref, second_ref, twr_ref, twi_ref, y_hbm, v_ref, y_ref, sems
):
    groups, chans, rows = y_ref.shape
    h = rows // 2
    twr, twi = twr_ref[...], twi_ref[...]
    copies = [
        pltpu.make_async_copy(rest_ref, y_hbm.at[:, :, pl.ds(rows, h)], sems.at[0]),
        pltpu.make_async_copy(y_ref, y_hbm.at[:, :, pl.ds(0, rows)], sems.at[1]),
    ]
    copies[0].start()
    even, odd = (dot(products(spec_ref[0, parity], spec_ref[1, parity], h, True), second_ref[1, parity]) for parity in (0, 1))
    y_ref[...] = signal(scale, even, odd, first_t_ref, twr, twi, v_ref)
    copies[1].start()
    for copy in copies:
        copy.wait()


class Writer:
    def __init__(self, outs, held, sems):
        self.outs, self.held, self.sems, self.copies = outs, held, sems, []

    def put(self, i, p, block):
        step = self.held.shape[2]
        self.held[i, p] = block.astype(BF16)
        copy = pltpu.make_async_copy(self.held.at[i, p], self.outs[i].at[pl.ds(p * step, step)], self.sems.at[i, p])
        copy.start()
        self.copies.append(copy)

    def wait(self):
        for copy in self.copies:
            copy.wait()


def gate_kernel(*refs):
    arrived = refs[:4]
    y_ref, q_ref, k_ref, v_ref, og_ref, bias_ref, mixed_hbm, qg_hbm, kg_hbm, vg_hbm, fg_hbm, x_ref, held, sems = refs[4:]
    owners, chans, _ = x_ref.shape
    writer = Writer((mixed_hbm, qg_hbm, kg_hbm, vg_hbm, fg_hbm), held, sems)
    parts, step = held.shape[1:3]
    bias = bias_ref[...]

    def take(ref, p):
        return ref[:, :, p * step : (p + 1) * step].reshape(owners * chans, step).T

    for p in range(parts):
        writer.put(4, p, take(y_ref, p))
    gather(lax.axis_index("context"), arrived, x_ref)
    for p in range(parts):
        span = slice(p * step, (p + 1) * step)
        q, k, v, og = q_ref[span], k_ref[span], v_ref[span], og_ref[span]
        pre_gate = take(x_ref, p).astype(F32) + bias * (k * v).astype(F32)
        writer.put(0, p, q.astype(F32) * pre_gate)
        writer.put(1, p, og.astype(F32) * pre_gate)
        back = take((x_ref, y_ref)[p], parts)
        gated_grad = back.astype(F32) + bias * (og * q).astype(F32)
        writer.put(2, p, gated_grad * v.astype(F32))
        writer.put(3, p, gated_grad * k.astype(F32))
    writer.wait()


def local(q_gate, k_gate, v_input, filter_taps, skip_bias, out_grad):
    groups = lax.axis_size("context")
    rows, width = q_gate.shape
    chans = width // groups
    order = device_order(groups)
    seq = groups * rows
    scale = 2.0 / (2 * seq) / math.sqrt(seq)
    messages = jax.ShapeDtypeStruct((groups, 3 * chans, rows), BF16)
    whole = jax.ShapeDtypeStruct((rows, width), BF16)
    limit = pltpu.CompilerParams(vmem_limit_bytes=48 * 1024 * 1024)
    far = pl.BlockSpec(memory_space=pltpu.HBM)
    near = pl.BlockSpec(memory_space=pltpu.VMEM)

    def swap(block):
        return lax.all_to_all(
            block, "context", split_axis=0, concat_axis=0, tiled=True, axis_index_groups=[order]
        )

    block = (chans, rows + rows // 2)
    bins = (chans * groups, rows)

    def call(kernel, name, out_shape, scratch_shapes=(), weight=0, **more):
        if weight:
            more["cost_estimate"] = pl.CostEstimate(flops=weight, bytes_accessed=weight, transcendentals=0)
        return pl.pallas_call(
            kernel, out_shape=out_shape, scratch_shapes=list(scratch_shapes), compiler_params=limit, name=name, **more
        )

    def shape(*dims):
        return jax.ShapeDtypeStruct(dims, BF16)

    def travel(own, other, after, weight):
        other = send(other, 0, 0, 1)
        leaving = call(
            along_z_kernel,
            "along_z",
            [shape(2, 4, *own.shape[2:])] * 3,
            weight=weight,
            in_specs=[near] * 2 + [pl.BlockSpec(memory_space=pl.ANY)],
            out_specs=[near] * 3,
        )(own, other, after)
        arrived = [None] * 3
        for dz in ZORDER:
            arrived[dz - 1] = send(leaving[dz - 1], dz, 0, 0)
        kept, *leaving = call(along_x_kernel, "along_x", [shape(4, 2, *own.shape[2:])] * 4, weight=weight)(
            own, other, *arrived
        )
        return [kept] + [send(part, 0, dx, 0) for dx, part in enumerate(leaving, start=1)]

    first, first_t, second, twr, twi = make_tables(order, rows)
    def keep(*arrays):
        return [pltpu.with_memory_space_constraint(x, pltpu.HBM) for x in arrays]

    one, half = (chans, rows), (chans, rows // 2)
    own, other, rest = call(
        pack_early_kernel,
        "pack_early",
        [pltpu.VMEM((4, 4, *block), BF16)] * 2 + [pltpu.VMEM((groups, *half), BF16)],
        [pltpu.VMEM((3, rows, width), BF16), pltpu.VMEM((groups, *block), BF16), pltpu.SemaphoreType.DMA((3,))],
        in_specs=[far] * 3,
        out_specs=[near] * 3,
    )(*keep(filter_taps, k_gate, v_input))
    sent = call(
        pack_late_kernel,
        "pack_late",
        shape(groups, *block),
        [pltpu.VMEM((2, rows, width), BF16), pltpu.VMEM((groups, *one), BF16), pltpu.SemaphoreType.DMA((4,))],
        in_specs=[far] * 2 + [near],
        out_specs=far,
    )(*keep(q_gate, out_grad), rest)
    taps, part = call(
        filter_kernel,
        "filter_spectrum",
        [jax.ShapeDtypeStruct((2, *bins), F32), shape(groups, *half)],
        [pltpu.VMEM((groups, *block), BF16), pltpu.VMEM((2, *bins), BF16)],
        weight=WEIGHT1,
    )(*travel(own, other, sent, WEIGHT1), first, second, twr, twi)
    items = swap(sent)
    own, other, rest, spec = call(
        functools.partial(forward_kernel, scale),
        "forward",
        [shape(4, 4, *block)] * 2
        + [shape(groups, *half), jax.ShapeDtypeStruct((2, 2, *bins), F32)],
        [
            pltpu.VMEM((2, 2, *bins), BF16),
            pltpu.VMEM((2, chans, 2 * groups, rows), BF16),
            pltpu.VMEM((groups, *block), BF16),
        ],
    )(items, taps, part, first, first_t, second, twr, twi)
    terms = call(
        functools.partial(backward_kernel, scale),
        "backward",
        shape(groups, *block),
        [
            pltpu.VMEM((chans, 2 * groups, rows), BF16),
            pltpu.VMEM((groups, *one), BF16),
            pltpu.SemaphoreType.DMA((2,)),
        ],
        in_specs=[near] * 6,
        out_specs=far,
    )(spec, rest, first_t, second, twr, twi)
    arrived = travel(own, other, terms, WEIGHT)
    parts = 2
    return call(
        gate_kernel,
        "gate",
        [whole] * 5,
        [
            pltpu.VMEM((groups, *block), BF16),
            pltpu.VMEM((5, parts, rows // parts, width), BF16),
            pltpu.SemaphoreType.DMA((5, parts)),
        ],
        in_specs=[near] * 10,
        out_specs=[far] * 5,
    )(*arrived, swap(terms), q_gate, k_gate, v_input, out_grad, skip_bias[None, :])


def solution(mesh):
    spec = P("context", "tensor")
    return jax.shard_map(
        local,
        mesh=mesh,
        in_specs=(spec, spec, spec, spec, P("tensor"), spec),
        out_specs=(spec,) * 5,
        check_vma=False,
    )
```

```python
import functools
import math

import jax
import jax.numpy as jnp
import ml_dtypes
import numpy as np
from jax import lax
from jax.experimental import pallas as pl
from jax.experimental.pallas import tpu as pltpu
from jax.sharding import PartitionSpec as P

BF16 = jnp.bfloat16
ZORDER = (1, 2, 3)
F32 = jnp.float32
WEIGHT1 = 8 * 10**9
WEIGHT = 8 * 10**9


QUARTERS = 4


def place(here):
    along = 4
    return here // (2 * along), here // 2 % along, here % 2


def block_of(here, dz, dx, dc):
    z, x, c = place(here)
    z = z ^ dz
    return (((x + dx) % 4) * 2 + (c ^ dc)) * 4 + (z ^ (1 - z // 2))


def device_order(groups):
    return sorted(range(groups), key=lambda here: block_of(here, 0, 0, 0))


def send(block, dz, dx, dc):
    groups = lax.axis_size("context")
    order = device_order(groups)
    moves = [(here, order[block_of(here, dz, dx, dc)]) for here in range(groups)]
    return lax.ppermute(block, "context", moves)


def make_tables(order, rows):
    groups = len(order)
    length = 2 * groups * rows
    a = np.array(order)[None, :]
    b = np.arange(rows)[None, :]
    half = np.arange(groups)[:, None] + 0.5
    theta = 2.0 * math.pi * a * half / (2 * groups)
    first = np.concatenate([np.cos(theta), -np.sin(theta)], axis=0)
    psi = 2.0 * math.pi * b * half / length
    low = np.arange(rows // 2)[:, None]
    m = np.arange(rows // 2)[None, :]
    second = []
    for parity in (0, 1):
        phi = 2.0 * math.pi * ((low * (2 * m + parity)) % rows) / rows
        second.append(np.block([[np.cos(phi), -np.sin(phi)], [np.sin(phi), np.cos(phi)]]))
    second = np.stack(second)
    narrow = ml_dtypes.bfloat16
    return (
        first.astype(narrow),
        np.ascontiguousarray(first.T).astype(narrow),
        np.stack([second, second.transpose(0, 2, 1)]).astype(narrow),
        np.cos(psi).astype(np.float32),
        (-np.sin(psi)).astype(np.float32),
    )


def halve(me, blocks, own_ref, other_ref):
    for dz in range(4):
        for dx in range(4):
            own_ref[dz, dx] = blocks[block_of(me, dz, dx, 0)]
            other_ref[dz, dx] = blocks[block_of(me, dz, dx, 1)]


def turn(block, chans):
    rows, width = block.shape
    return block.T.reshape(width // chans, chans, rows)


def pack_early_kernel(f_hbm, k_hbm, v_hbm, own_ref, other_ref, rest_ref, held, turned, sems):
    owners, chans, h = rest_ref.shape
    rows = 2 * h
    copies = [pltpu.make_async_copy(src, held.at[i], sems.at[i]) for i, src in enumerate((f_hbm, k_hbm, v_hbm))]
    for copy in copies:
        copy.start()
    me = lax.axis_index("context")
    copies[0].wait()
    turned[:, :, :rows] = turn(held[0], chans)
    copies[1].wait()
    copies[2].wait()
    gated = turn(held[1] * held[2], chans)
    turned[:, :, rows:] = gated[:, :, :h]
    rest_ref[...] = gated[:, :, h:]
    halve(me, turned, own_ref, other_ref)


def pack_late_kernel(q_hbm, og_hbm, rest_ref, out_hbm, held, out_ref, sems):
    owners, chans, rows = out_ref.shape
    copies = [pltpu.make_async_copy(src, held.at[i], sems.at[i]) for i, src in enumerate((q_hbm, og_hbm))]
    leaving = [
        pltpu.make_async_copy(rest_ref, out_hbm.at[:, :, pl.ds(rows, rows // 2)], sems.at[2]),
        pltpu.make_async_copy(out_ref, out_hbm.at[:, :, pl.ds(0, rows)], sems.at[3]),
    ]
    for copy in copies:
        copy.start()
    leaving[0].start()
    for copy in copies:
        copy.wait()
    out_ref[...] = turn(held[0] * held[1], chans)
    leaving[1].start()
    for copy in leaving:
        copy.wait()


def along_z_kernel(own_ref, other_ref, after_ref, *outs):
    for dz, out in enumerate(outs, start=1):
        for sc, ref in enumerate((own_ref, other_ref)):
            for dx in range(4):
                out[sc, dx] = ref[dz, dx]


def along_x_kernel(own_ref, other_ref, *refs):
    arrived, outs = refs[:3], refs[3:]
    for dx, out in enumerate(outs):
        for sc, ref in enumerate((own_ref, other_ref)):
            out[0, sc] = ref[0, dx]
            for dz, ref in enumerate(arrived, start=1):
                out[dz, sc] = ref[sc, dx]


def gather(me, arrived, x_ref):
    for dx, ref in enumerate(arrived):
        for dz in range(4):
            for sc in range(2):
                x_ref[block_of(me, dz, -dx, sc)] = ref[dz, sc]


def dot(a, b):
    return jnp.dot(a, b, preferred_element_type=F32)


def spectrum(items, first_ref, second_ref, twr, twi, t_ref):
    chans, groups, rows = items.shape
    h = rows // 2
    for c in range(chans):
        part = dot(first_ref[...], items[c])
        real, imag = part[:groups], part[groups:]
        tr, ti = real * twr - imag * twi, real * twi + imag * twr
        lines = slice(c * groups, (c + 1) * groups)
        t_ref[0, lines, :h] = (tr[:, :h] + tr[:, h:]).astype(BF16)
        t_ref[0, lines, h:] = (ti[:, :h] + ti[:, h:]).astype(BF16)
        t_ref[1, lines, :h] = (tr[:, :h] - tr[:, h:]).astype(BF16)
        t_ref[1, lines, h:] = (ti[:, :h] - ti[:, h:]).astype(BF16)
    return [dot(t_ref[parity], second_ref[0, parity]) for parity in (0, 1)]


def products(left, right, h, conjugate):
    lr, li, rr, ri = left[:, :h], left[:, h:], right[:, :h], right[:, h:]
    if conjugate:
        real, imag = lr * rr + li * ri, lr * ri - li * rr
    else:
        real, imag = lr * rr - li * ri, lr * ri + li * rr
    return jnp.concatenate([real.astype(BF16), imag.astype(BF16)], axis=1)


def signal(scale, even, odd, first_t_ref, twr, twi, v_ref):
    chans, twice, rows = v_ref.shape
    groups = twice // 2
    h = rows // 2
    even, odd = even.reshape(chans, groups, rows), odd.reshape(chans, groups, rows)
    for part, lanes in ((even + odd, slice(0, h)), (even - odd, slice(h, rows))):
        real, imag = part[:, :, :h], part[:, :, h:]
        v_ref[:, :groups, lanes] = (real * twr[:, lanes] + imag * twi[:, lanes]).astype(BF16)
        v_ref[:, groups:, lanes] = (imag * twr[:, lanes] - real * twi[:, lanes]).astype(BF16)
    out = jnp.stack([dot(first_t_ref[...], v_ref[c]) * scale for c in range(chans)], axis=0)
    return jnp.swapaxes(out.astype(BF16), 0, 1)


def forward_kernel(scale, *refs):
    arrived = refs[:4]
    x_ref, first_ref, first_t_ref, second_ref, twr_ref, twi_ref = refs[4:10]
    own_ref, other_ref, rest_ref, spec_ref, t_ref, v_ref, y_ref = refs[10:]
    rows = twr_ref.shape[1]
    h = rows // 2
    twr, twi = twr_ref[...], twi_ref[...]
    gather(lax.axis_index("context"), arrived, y_ref)
    gated = jnp.concatenate([y_ref[:, :, rows:], x_ref[:, :, rows:]], axis=2)
    taps, gated, delta = (
        spectrum(jnp.swapaxes(block, 0, 1), first_ref, second_ref, twr, twi, t_ref.at[s])
        for s, block in enumerate((y_ref[:, :, :rows], gated, x_ref[:, :, :rows]))
    )
    for parity in (0, 1):
        spec_ref[0, parity] = gated[parity]
        spec_ref[1, parity] = delta[parity]
    even, odd = (dot(products(gated[parity], taps[parity], h, False), second_ref[1, parity]) for parity in (0, 1))
    y_ref[:, :, :rows] = signal(scale, even, odd, first_t_ref, twr, twi, v_ref.at[0])
    even, odd = (dot(products(taps[parity], delta[parity], h, True), second_ref[1, parity]) for parity in (0, 1))
    back = signal(scale, even, odd, first_t_ref, twr, twi, v_ref.at[1])
    y_ref[:, :, rows:] = back[:, :, :h]
    rest_ref[...] = back[:, :, h:]
    halve(lax.axis_index("context"), y_ref, own_ref, other_ref)


def backward_kernel(
    scale, spec_ref, rest_ref, first_t_ref, second_ref, twr_ref, twi_ref, y_hbm, v_ref, y_ref, sems
):
    groups, chans, rows = y_ref.shape
    h = rows // 2
    twr, twi = twr_ref[...], twi_ref[...]
    copies = [
        pltpu.make_async_copy(rest_ref, y_hbm.at[:, :, pl.ds(rows, h)], sems.at[0]),
        pltpu.make_async_copy(y_ref, y_hbm.at[:, :, pl.ds(0, rows)], sems.at[1]),
    ]
    copies[0].start()
    even, odd = (dot(products(spec_ref[0, parity], spec_ref[1, parity], h, True), second_ref[1, parity]) for parity in (0, 1))
    y_ref[...] = signal(scale, even, odd, first_t_ref, twr, twi, v_ref)
    copies[1].start()
    for copy in copies:
        copy.wait()


class Writer:
    def __init__(self, outs, held, sems):
        self.outs, self.held, self.sems, self.copies = outs, held, sems, []

    def put(self, i, p, block):
        step = self.held.shape[2]
        self.held[i, p] = block.astype(BF16)
        copy = pltpu.make_async_copy(self.held.at[i, p], self.outs[i].at[pl.ds(p * step, step)], self.sems.at[i, p])
        copy.start()
        self.copies.append(copy)

    def wait(self):
        for copy in self.copies:
            copy.wait()


def gate_kernel(*refs):
    arrived = refs[:4]
    y_ref, q_ref, k_ref, v_ref, og_ref, bias_ref, mixed_hbm, qg_hbm, kg_hbm, vg_hbm, fg_hbm, x_ref, held, sems = refs[4:]
    owners, chans, _ = x_ref.shape
    writer = Writer((mixed_hbm, qg_hbm, kg_hbm, vg_hbm, fg_hbm), held, sems)
    parts, step = held.shape[1:3]
    bias = bias_ref[...]

    def take(ref, p):
        return ref[:, :, p * step : (p + 1) * step].reshape(owners * chans, step).T

    for p in range(parts):
        writer.put(4, p, take(y_ref, p))
    gather(lax.axis_index("context"), arrived, x_ref)
    for p in range(parts):
        span = slice(p * step, (p + 1) * step)
        q, k, v, og = q_ref[span], k_ref[span], v_ref[span], og_ref[span]
        pre_gate = take(x_ref, p).astype(F32) + bias * (k * v).astype(F32)
        writer.put(0, p, q.astype(F32) * pre_gate)
        writer.put(1, p, og.astype(F32) * pre_gate)
        back = take((x_ref, y_ref)[p], parts)
        gated_grad = back.astype(F32) + bias * (og * q).astype(F32)
        writer.put(2, p, gated_grad * v.astype(F32))
        writer.put(3, p, gated_grad * k.astype(F32))
    writer.wait()


def local(q_gate, k_gate, v_input, filter_taps, skip_bias, out_grad):
    groups = lax.axis_size("context")
    rows, width = q_gate.shape
    chans = width // groups
    order = device_order(groups)
    seq = groups * rows
    scale = 2.0 / (2 * seq) / math.sqrt(seq)
    messages = jax.ShapeDtypeStruct((groups, 3 * chans, rows), BF16)
    whole = jax.ShapeDtypeStruct((rows, width), BF16)
    limit = pltpu.CompilerParams(vmem_limit_bytes=48 * 1024 * 1024)
    far = pl.BlockSpec(memory_space=pltpu.HBM)
    near = pl.BlockSpec(memory_space=pltpu.VMEM)

    def swap(block):
        return lax.all_to_all(
            block, "context", split_axis=0, concat_axis=0, tiled=True, axis_index_groups=[order]
        )

    block = (chans, rows + rows // 2)
    bins = (chans * groups, rows)

    def call(kernel, name, out_shape, scratch_shapes=(), weight=0, **more):
        if weight:
            more["cost_estimate"] = pl.CostEstimate(flops=weight, bytes_accessed=weight, transcendentals=0)
        return pl.pallas_call(
            kernel, out_shape=out_shape, scratch_shapes=list(scratch_shapes), compiler_params=limit, name=name, **more
        )

    def shape(*dims):
        return jax.ShapeDtypeStruct(dims, BF16)

    def travel(own, other, after, weight):
        other = send(other, 0, 0, 1)
        leaving = call(
            along_z_kernel,
            "along_z",
            [shape(2, 4, *own.shape[2:])] * 3,
            weight=weight,
            in_specs=[near] * 2 + [pl.BlockSpec(memory_space=pl.ANY)],
            out_specs=[near] * 3,
        )(own, other, after)
        arrived = [None] * 3
        for dz in ZORDER:
            arrived[dz - 1] = send(leaving[dz - 1], dz, 0, 0)
        kept, *leaving = call(along_x_kernel, "along_x", [shape(4, 2, *own.shape[2:])] * 4, weight=weight)(
            own, other, *arrived
        )
        return [kept] + [send(part, 0, dx, 0) for dx, part in enumerate(leaving, start=1)]

    first, first_t, second, twr, twi = make_tables(order, rows)
    def keep(*arrays):
        return [pltpu.with_memory_space_constraint(x, pltpu.HBM) for x in arrays]

    one, half = (chans, rows), (chans, rows // 2)
    own, other, rest = call(
        pack_early_kernel,
        "pack_early",
        [pltpu.VMEM((4, 4, *block), BF16)] * 2 + [pltpu.VMEM((groups, *half), BF16)],
        [pltpu.VMEM((3, rows, width), BF16), pltpu.VMEM((groups, *block), BF16), pltpu.SemaphoreType.DMA((3,))],
        in_specs=[far] * 3,
        out_specs=[near] * 3,
    )(*keep(filter_taps, k_gate, v_input))
    sent = call(
        pack_late_kernel,
        "pack_late",
        shape(groups, *block),
        [pltpu.VMEM((2, rows, width), BF16), pltpu.VMEM((groups, *one), BF16), pltpu.SemaphoreType.DMA((4,))],
        in_specs=[far] * 2 + [near],
        out_specs=far,
    )(*keep(q_gate, out_grad), rest)
    early = travel(own, other, sent, WEIGHT1)
    items = swap(sent)
    own, other, rest, spec = call(
        functools.partial(forward_kernel, scale),
        "forward",
        [shape(4, 4, *block)] * 2
        + [shape(groups, *half), jax.ShapeDtypeStruct((2, 2, *bins), F32)],
        [
            pltpu.VMEM((3, 2, *bins), BF16),
            pltpu.VMEM((2, chans, 2 * groups, rows), BF16),
            pltpu.VMEM((groups, *block), BF16),
        ],
    )(*early, items, first, first_t, second, twr, twi)
    terms = call(
        functools.partial(backward_kernel, scale),
        "backward",
        shape(groups, *block),
        [
            pltpu.VMEM((chans, 2 * groups, rows), BF16),
            pltpu.VMEM((groups, *one), BF16),
            pltpu.SemaphoreType.DMA((2,)),
        ],
        in_specs=[near] * 6,
        out_specs=far,
    )(spec, rest, first_t, second, twr, twi)
    arrived = travel(own, other, terms, WEIGHT)
    parts = 2
    return call(
        gate_kernel,
        "gate",
        [whole] * 5,
        [
            pltpu.VMEM((groups, *block), BF16),
            pltpu.VMEM((5, parts, rows // parts, width), BF16),
            pltpu.SemaphoreType.DMA((5, parts)),
        ],
        in_specs=[near] * 10,
        out_specs=[far] * 5,
    )(*arrived, swap(terms), q_gate, k_gate, v_input, out_grad, skip_bias[None, :])


def solution(mesh):
    spec = P("context", "tensor")
    return jax.shard_map(
        local,
        mesh=mesh,
        in_specs=(spec, spec, spec, spec, P("tensor"), spec),
        out_specs=(spec,) * 5,
        check_vma=False,
    )
```

```python
import functools
import math

import jax
import jax.numpy as jnp
import ml_dtypes
import numpy as np
from jax import lax
from jax.experimental import pallas as pl
from jax.experimental.pallas import tpu as pltpu
from jax.sharding import PartitionSpec as P

BF16 = jnp.bfloat16
ZORDER = (1, 2, 3)
F32 = jnp.float32
WEIGHT1 = 8 * 10**9
WEIGHT = 8 * 10**9


QUARTERS = 4


def place(here):
    along = 4
    return here // (2 * along), here // 2 % along, here % 2


def block_of(here, dz, dx, dc):
    z, x, c = place(here)
    z = z ^ dz
    return (((x + dx) % 4) * 2 + (c ^ dc)) * 4 + (z ^ (1 - z // 2))


def device_order(groups):
    return sorted(range(groups), key=lambda here: block_of(here, 0, 0, 0))


def send(block, dz, dx, dc):
    groups = lax.axis_size("context")
    order = device_order(groups)
    moves = [(here, order[block_of(here, dz, dx, dc)]) for here in range(groups)]
    return lax.ppermute(block, "context", moves)


def make_tables(order, rows):
    groups = len(order)
    length = 2 * groups * rows
    a = np.array(order)[None, :]
    b = np.arange(rows)[None, :]
    half = np.arange(groups)[:, None] + 0.5
    theta = 2.0 * math.pi * a * half / (2 * groups)
    first = np.concatenate([np.cos(theta), -np.sin(theta)], axis=0)
    psi = 2.0 * math.pi * b * half / length
    low = np.arange(rows // 2)[:, None]
    m = np.arange(rows // 2)[None, :]
    second = []
    for parity in (0, 1):
        phi = 2.0 * math.pi * ((low * (2 * m + parity)) % rows) / rows
        second.append(np.block([[np.cos(phi), -np.sin(phi)], [np.sin(phi), np.cos(phi)]]))
    second = np.stack(second)
    narrow = ml_dtypes.bfloat16
    return (
        first.astype(narrow),
        np.ascontiguousarray(first.T).astype(narrow),
        np.stack([second, second.transpose(0, 2, 1)]).astype(narrow),
        np.cos(psi).astype(np.float32),
        (-np.sin(psi)).astype(np.float32),
    )


def halve(me, blocks, own_ref, other_ref):
    for dz in range(4):
        for dx in range(4):
            own_ref[dz, dx] = blocks[block_of(me, dz, dx, 0)]
            other_ref[dz, dx] = blocks[block_of(me, dz, dx, 1)]


def turn(block, chans):
    rows, width = block.shape
    return block.T.reshape(width // chans, chans, rows)


def pack_early_kernel(f_hbm, k_hbm, v_hbm, own_ref, other_ref, rest_ref, held, turned, sems):
    owners, chans, h = rest_ref.shape
    rows = 2 * h
    copies = [pltpu.make_async_copy(src, held.at[i], sems.at[i]) for i, src in enumerate((f_hbm, k_hbm, v_hbm))]
    for copy in copies:
        copy.start()
    me = lax.axis_index("context")
    copies[0].wait()
    turned[:, :, :rows] = turn(held[0], chans)
    copies[1].wait()
    copies[2].wait()
    gated = turn(held[1] * held[2], chans)
    turned[:, :, rows:] = gated[:, :, :h]
    rest_ref[...] = gated[:, :, h:]
    halve(me, turned, own_ref, other_ref)


def pack_late_kernel(q_hbm, og_hbm, rest_ref, out_hbm, held, out_ref, sems):
    owners, chans, rows = out_ref.shape
    copies = [pltpu.make_async_copy(src, held.at[i], sems.at[i]) for i, src in enumerate((q_hbm, og_hbm))]
    leaving = [
        pltpu.make_async_copy(rest_ref, out_hbm.at[:, :, pl.ds(rows, rows // 2)], sems.at[2]),
        pltpu.make_async_copy(out_ref, out_hbm.at[:, :, pl.ds(0, rows)], sems.at[3]),
    ]
    for copy in copies:
        copy.start()
    leaving[0].start()
    for copy in copies:
        copy.wait()
    out_ref[...] = turn(held[0] * held[1], chans)
    leaving[1].start()
    for copy in leaving:
        copy.wait()


def along_z_kernel(own_ref, other_ref, after_ref, *outs):
    for dz, out in enumerate(outs, start=1):
        for sc, ref in enumerate((own_ref, other_ref)):
            for dx in range(4):
                out[sc, dx] = ref[dz, dx]


def along_x_kernel(own_ref, other_ref, *refs):
    arrived, outs = refs[:3], refs[3:]
    for dx, out in enumerate(outs):
        for sc, ref in enumerate((own_ref, other_ref)):
            out[0, sc] = ref[0, dx]
            for dz, ref in enumerate(arrived, start=1):
                out[dz, sc] = ref[sc, dx]


def gather(me, arrived, x_ref):
    for dx, ref in enumerate(arrived):
        for dz in range(4):
            for sc in range(2):
                x_ref[block_of(me, dz, -dx, sc)] = ref[dz, sc]


def dot(a, b):
    return jnp.dot(a, b, preferred_element_type=F32)


def spectrum(items, first_ref, second_ref, twr, twi, t_ref):
    chans, groups, rows = items.shape
    h = rows // 2
    for c in range(chans):
        part = dot(first_ref[...], items[c])
        real, imag = part[:groups], part[groups:]
        tr, ti = real * twr - imag * twi, real * twi + imag * twr
        lines = slice(c * groups, (c + 1) * groups)
        t_ref[0, lines, :h] = (tr[:, :h] + tr[:, h:]).astype(BF16)
        t_ref[0, lines, h:] = (ti[:, :h] + ti[:, h:]).astype(BF16)
        t_ref[1, lines, :h] = (tr[:, :h] - tr[:, h:]).astype(BF16)
        t_ref[1, lines, h:] = (ti[:, :h] - ti[:, h:]).astype(BF16)
    return [dot(t_ref[parity], second_ref[0, parity]) for parity in (0, 1)]


def products(left, right, h, conjugate):
    lr, li, rr, ri = left[:, :h], left[:, h:], right[:, :h], right[:, h:]
    if conjugate:
        real, imag = lr * rr + li * ri, lr * ri - li * rr
    else:
        real, imag = lr * rr - li * ri, lr * ri + li * rr
    return jnp.concatenate([real.astype(BF16), imag.astype(BF16)], axis=1)


def signal(scale, even, odd, first_t_ref, twr, twi, v_ref):
    chans, twice, rows = v_ref.shape
    groups = twice // 2
    h = rows // 2
    even, odd = even.reshape(chans, groups, rows), odd.reshape(chans, groups, rows)
    for part, lanes in ((even + odd, slice(0, h)), (even - odd, slice(h, rows))):
        real, imag = part[:, :, :h], part[:, :, h:]
        v_ref[:, :groups, lanes] = (real * twr[:, lanes] + imag * twi[:, lanes]).astype(BF16)
        v_ref[:, groups:, lanes] = (imag * twr[:, lanes] - real * twi[:, lanes]).astype(BF16)
    out = jnp.stack([dot(first_t_ref[...], v_ref[c]) * scale for c in range(chans)], axis=0)
    return jnp.swapaxes(out.astype(BF16), 0, 1)


def forward_kernel(scale, *refs):
    arrived = refs[:4]
    x_ref, first_ref, first_t_ref, second_ref, twr_ref, twi_ref = refs[4:10]
    own_ref, other_ref, rest_ref, prod_ref, t_ref, v_ref, y_ref = refs[10:]
    rows = twr_ref.shape[1]
    h = rows // 2
    twr, twi = twr_ref[...], twi_ref[...]
    gather(lax.axis_index("context"), arrived, y_ref)
    gated = jnp.concatenate([y_ref[:, :, rows:], x_ref[:, :, rows:]], axis=2)
    taps, gated, delta = (
        spectrum(jnp.swapaxes(block, 0, 1), first_ref, second_ref, twr, twi, t_ref.at[s])
        for s, block in enumerate((y_ref[:, :, :rows], gated, x_ref[:, :, :rows]))
    )
    for parity in (0, 1):
        prod_ref[parity] = products(gated[parity], delta[parity], h, True)
    even, odd = (dot(products(gated[parity], taps[parity], h, False), second_ref[1, parity]) for parity in (0, 1))
    y_ref[:, :, :rows] = signal(scale, even, odd, first_t_ref, twr, twi, v_ref.at[0])
    even, odd = (dot(products(taps[parity], delta[parity], h, True), second_ref[1, parity]) for parity in (0, 1))
    back = signal(scale, even, odd, first_t_ref, twr, twi, v_ref.at[1])
    y_ref[:, :, rows:] = back[:, :, :h]
    rest_ref[...] = back[:, :, h:]
    halve(lax.axis_index("context"), y_ref, own_ref, other_ref)


def backward_kernel(
    scale, prod_ref, rest_ref, first_t_ref, second_ref, twr_ref, twi_ref, y_hbm, v_ref, y_ref, sems
):
    groups, chans, rows = y_ref.shape
    h = rows // 2
    twr, twi = twr_ref[...], twi_ref[...]
    copies = [
        pltpu.make_async_copy(rest_ref, y_hbm.at[:, :, pl.ds(rows, h)], sems.at[0]),
        pltpu.make_async_copy(y_ref, y_hbm.at[:, :, pl.ds(0, rows)], sems.at[1]),
    ]
    copies[0].start()
    even, odd = (dot(prod_ref[parity], second_ref[1, parity]) for parity in (0, 1))
    y_ref[...] = signal(scale, even, odd, first_t_ref, twr, twi, v_ref)
    copies[1].start()
    for copy in copies:
        copy.wait()


class Writer:
    def __init__(self, outs, held, sems):
        self.outs, self.held, self.sems, self.copies = outs, held, sems, []

    def put(self, i, p, block):
        step = self.held.shape[2]
        self.held[i, p] = block.astype(BF16)
        copy = pltpu.make_async_copy(self.held.at[i, p], self.outs[i].at[pl.ds(p * step, step)], self.sems.at[i, p])
        copy.start()
        self.copies.append(copy)

    def wait(self):
        for copy in self.copies:
            copy.wait()


def gate_kernel(*refs):
    arrived = refs[:4]
    y_ref, q_ref, k_ref, v_ref, og_ref, bias_ref, mixed_hbm, qg_hbm, kg_hbm, vg_hbm, fg_hbm, x_ref, held, sems = refs[4:]
    owners, chans, _ = x_ref.shape
    writer = Writer((mixed_hbm, qg_hbm, kg_hbm, vg_hbm, fg_hbm), held, sems)
    parts, step = held.shape[1:3]
    bias = bias_ref[...]

    def take(ref, p):
        return ref[:, :, p * step : (p + 1) * step].reshape(owners * chans, step).T

    for p in range(parts):
        writer.put(4, p, take(y_ref, p))
    gather(lax.axis_index("context"), arrived, x_ref)
    for p in range(parts):
        span = slice(p * step, (p + 1) * step)
        q, k, v, og = q_ref[span], k_ref[span], v_ref[span], og_ref[span]
        pre_gate = take(x_ref, p).astype(F32) + bias * (k * v).astype(F32)
        writer.put(0, p, q.astype(F32) * pre_gate)
        writer.put(1, p, og.astype(F32) * pre_gate)
        back = take((x_ref, y_ref)[p], parts)
        gated_grad = back.astype(F32) + bias * (og * q).astype(F32)
        writer.put(2, p, gated_grad * v.astype(F32))
        writer.put(3, p, gated_grad * k.astype(F32))
    writer.wait()


def local(q_gate, k_gate, v_input, filter_taps, skip_bias, out_grad):
    groups = lax.axis_size("context")
    rows, width = q_gate.shape
    chans = width // groups
    order = device_order(groups)
    seq = groups * rows
    scale = 2.0 / (2 * seq) / math.sqrt(seq)
    messages = jax.ShapeDtypeStruct((groups, 3 * chans, rows), BF16)
    whole = jax.ShapeDtypeStruct((rows, width), BF16)
    limit = pltpu.CompilerParams(vmem_limit_bytes=48 * 1024 * 1024)
    far = pl.BlockSpec(memory_space=pltpu.HBM)
    near = pl.BlockSpec(memory_space=pltpu.VMEM)

    def swap(block):
        return lax.all_to_all(
            block, "context", split_axis=0, concat_axis=0, tiled=True, axis_index_groups=[order]
        )

    block = (chans, rows + rows // 2)
    bins = (chans * groups, rows)

    def call(kernel, name, out_shape, scratch_shapes=(), weight=0, **more):
        if weight:
            more["cost_estimate"] = pl.CostEstimate(flops=weight, bytes_accessed=weight, transcendentals=0)
        return pl.pallas_call(
            kernel, out_shape=out_shape, scratch_shapes=list(scratch_shapes), compiler_params=limit, name=name, **more
        )

    def shape(*dims):
        return jax.ShapeDtypeStruct(dims, BF16)

    def travel(own, other, after, weight):
        other = send(other, 0, 0, 1)
        leaving = call(
            along_z_kernel,
            "along_z",
            [shape(2, 4, *own.shape[2:])] * 3,
            weight=weight,
            in_specs=[near] * 2 + [pl.BlockSpec(memory_space=pl.ANY)],
            out_specs=[near] * 3,
        )(own, other, after)
        arrived = [None] * 3
        for dz in ZORDER:
            arrived[dz - 1] = send(leaving[dz - 1], dz, 0, 0)
        kept, *leaving = call(along_x_kernel, "along_x", [shape(4, 2, *own.shape[2:])] * 4, weight=weight)(
            own, other, *arrived
        )
        return [kept] + [send(part, 0, dx, 0) for dx, part in enumerate(leaving, start=1)]

    first, first_t, second, twr, twi = make_tables(order, rows)
    def keep(*arrays):
        return [pltpu.with_memory_space_constraint(x, pltpu.HBM) for x in arrays]

    one, half = (chans, rows), (chans, rows // 2)
    own, other, rest = call(
        pack_early_kernel,
        "pack_early",
        [pltpu.VMEM((4, 4, *block), BF16)] * 2 + [pltpu.VMEM((groups, *half), BF16)],
        [pltpu.VMEM((3, rows, width), BF16), pltpu.VMEM((groups, *block), BF16), pltpu.SemaphoreType.DMA((3,))],
        in_specs=[far] * 3,
        out_specs=[near] * 3,
    )(*keep(filter_taps, k_gate, v_input))
    sent = call(
        pack_late_kernel,
        "pack_late",
        shape(groups, *block),
        [pltpu.VMEM((2, rows, width), BF16), pltpu.VMEM((groups, *one), BF16), pltpu.SemaphoreType.DMA((4,))],
        in_specs=[far] * 2 + [near],
        out_specs=far,
    )(*keep(q_gate, out_grad), rest)
    early = travel(own, other, sent, WEIGHT1)
    items = swap(sent)
    own, other, rest, crossed = call(
        functools.partial(forward_kernel, scale),
        "forward",
        [shape(4, 4, *block)] * 2
        + [shape(groups, *half), shape(2, *bins)],
        [
            pltpu.VMEM((3, 2, *bins), BF16),
            pltpu.VMEM((2, chans, 2 * groups, rows), BF16),
            pltpu.VMEM((groups, *block), BF16),
        ],
    )(*early, items, first, first_t, second, twr, twi)
    terms = call(
        functools.partial(backward_kernel, scale),
        "backward",
        shape(groups, *block),
        [
            pltpu.VMEM((chans, 2 * groups, rows), BF16),
            pltpu.VMEM((groups, *one), BF16),
            pltpu.SemaphoreType.DMA((2,)),
        ],
        in_specs=[near] * 6,
        out_specs=far,
    )(crossed, rest, first_t, second, twr, twi)
    arrived = travel(own, other, terms, WEIGHT)
    parts = 2
    return call(
        gate_kernel,
        "gate",
        [whole] * 5,
        [
            pltpu.VMEM((groups, *block), BF16),
            pltpu.VMEM((5, parts, rows // parts, width), BF16),
            pltpu.SemaphoreType.DMA((5, parts)),
        ],
        in_specs=[near] * 10,
        out_specs=[far] * 5,
    )(*arrived, swap(terms), q_gate, k_gate, v_input, out_grad, skip_bias[None, :])


def solution(mesh):
    spec = P("context", "tensor")
    return jax.shard_map(
        local,
        mesh=mesh,
        in_specs=(spec, spec, spec, spec, P("tensor"), spec),
        out_specs=(spec,) * 5,
        check_vma=False,
    )
```

```python
import functools
import math

import jax
import jax.numpy as jnp
import ml_dtypes
import numpy as np
from jax import lax
from jax.experimental import pallas as pl
from jax.experimental.pallas import tpu as pltpu
from jax.sharding import PartitionSpec as P

BF16 = jnp.bfloat16
ZORDER = (1, 2, 3)
F32 = jnp.float32
WEIGHT1 = 8 * 10**9
WEIGHT = 8 * 10**9


QUARTERS = 4


def place(here):
    along = 4
    return here // (2 * along), here // 2 % along, here % 2


def block_of(here, dz, dx, dc):
    z, x, c = place(here)
    z = z ^ dz
    return (((x + dx) % 4) * 2 + (c ^ dc)) * 4 + (z ^ (1 - z // 2))


def device_order(groups):
    return sorted(range(groups), key=lambda here: block_of(here, 0, 0, 0))


def send(block, dz, dx, dc):
    groups = lax.axis_size("context")
    order = device_order(groups)
    moves = [(here, order[block_of(here, dz, dx, dc)]) for here in range(groups)]
    return lax.ppermute(block, "context", moves)


def make_tables(order, rows):
    groups = len(order)
    length = 2 * groups * rows
    a = np.array(order)[None, :]
    b = np.arange(rows)[None, :]
    half = np.arange(groups)[:, None] + 0.5
    theta = 2.0 * math.pi * a * half / (2 * groups)
    first = np.concatenate([np.cos(theta), -np.sin(theta)], axis=0)
    psi = 2.0 * math.pi * b * half / length
    low = np.arange(rows // 2)[:, None]
    m = np.arange(rows // 2)[None, :]
    second = []
    for parity in (0, 1):
        phi = 2.0 * math.pi * ((low * (2 * m + parity)) % rows) / rows
        second.append(np.block([[np.cos(phi), -np.sin(phi)], [np.sin(phi), np.cos(phi)]]))
    second = np.stack(second)
    narrow = ml_dtypes.bfloat16
    return (
        first.astype(narrow),
        np.ascontiguousarray(first.T).astype(narrow),
        np.stack([second, second.transpose(0, 2, 1)]).astype(narrow),
        np.cos(psi).astype(np.float32),
        (-np.sin(psi)).astype(np.float32),
    )


def halve(me, blocks, own_ref, other_ref):
    for dz in range(4):
        for dx in range(4):
            own_ref[dz, dx] = blocks[block_of(me, dz, dx, 0)]
            other_ref[dz, dx] = blocks[block_of(me, dz, dx, 1)]


def turn(block, chans):
    rows, width = block.shape
    return block.T.reshape(width // chans, chans, rows)


def pack_early_kernel(f_hbm, k_hbm, v_hbm, own_ref, other_ref, rest_ref, held, turned, sems):
    owners, chans, h = rest_ref.shape
    rows = 2 * h
    copies = [pltpu.make_async_copy(src, held.at[i], sems.at[i]) for i, src in enumerate((f_hbm, k_hbm, v_hbm))]
    for copy in copies:
        copy.start()
    me = lax.axis_index("context")
    copies[0].wait()
    turned[:, :, :rows] = turn(held[0], chans)
    copies[1].wait()
    copies[2].wait()
    gated = turn(held[1] * held[2], chans)
    turned[:, :, rows:] = gated[:, :, :h]
    rest_ref[...] = gated[:, :, h:]
    halve(me, turned, own_ref, other_ref)


def pack_late_kernel(q_hbm, og_hbm, rest_ref, out_hbm, held, out_ref, sems):
    owners, chans, rows = out_ref.shape
    copies = [pltpu.make_async_copy(src, held.at[i], sems.at[i]) for i, src in enumerate((q_hbm, og_hbm))]
    leaving = [
        pltpu.make_async_copy(rest_ref, out_hbm.at[:, :, pl.ds(rows, rows // 2)], sems.at[2]),
        pltpu.make_async_copy(out_ref, out_hbm.at[:, :, pl.ds(0, rows)], sems.at[3]),
    ]
    for copy in copies:
        copy.start()
    leaving[0].start()
    for copy in copies:
        copy.wait()
    out_ref[...] = turn(held[0] * held[1], chans)
    leaving[1].start()
    for copy in leaving:
        copy.wait()


def along_z_kernel(own_ref, other_ref, after_ref, *outs):
    for dz, out in enumerate(outs, start=1):
        for sc, ref in enumerate((own_ref, other_ref)):
            for dx in range(4):
                out[sc, dx] = ref[dz, dx]


def along_x_kernel(own_ref, other_ref, *refs):
    arrived, outs = refs[:3], refs[3:]
    for dx, out in enumerate(outs):
        for sc, ref in enumerate((own_ref, other_ref)):
            out[0, sc] = ref[0, dx]
            for dz, ref in enumerate(arrived, start=1):
                out[dz, sc] = ref[sc, dx]


def gather(me, arrived, x_ref):
    for dx, ref in enumerate(arrived):
        for dz in range(4):
            for sc in range(2):
                x_ref[block_of(me, dz, -dx, sc)] = ref[dz, sc]


def dot(a, b):
    return jnp.dot(a, b, preferred_element_type=F32)


def spectrum(items, first_ref, second_ref, twr, twi, t_ref):
    chans, groups, rows = items.shape
    h = rows // 2
    for c in range(chans):
        part = dot(first_ref[...], items[c])
        real, imag = part[:groups], part[groups:]
        tr, ti = real * twr - imag * twi, real * twi + imag * twr
        lines = slice(c * groups, (c + 1) * groups)
        t_ref[0, lines, :h] = (tr[:, :h] + tr[:, h:]).astype(BF16)
        t_ref[0, lines, h:] = (ti[:, :h] + ti[:, h:]).astype(BF16)
        t_ref[1, lines, :h] = (tr[:, :h] - tr[:, h:]).astype(BF16)
        t_ref[1, lines, h:] = (ti[:, :h] - ti[:, h:]).astype(BF16)
    return [dot(t_ref[parity], second_ref[0, parity]) for parity in (0, 1)]


def products(left, right, h, conjugate):
    lr, li, rr, ri = left[:, :h], left[:, h:], right[:, :h], right[:, h:]
    if conjugate:
        real, imag = lr * rr + li * ri, lr * ri - li * rr
    else:
        real, imag = lr * rr - li * ri, lr * ri + li * rr
    return jnp.concatenate([real.astype(BF16), imag.astype(BF16)], axis=1)


def signal(scale, even, odd, first_t_ref, twr, twi, v_ref):
    chans, twice, rows = v_ref.shape
    groups = twice // 2
    h = rows // 2
    even, odd = even.reshape(chans, groups, rows), odd.reshape(chans, groups, rows)
    twr, twi = twr * scale, twi * scale
    for part, lanes in ((even + odd, slice(0, h)), (even - odd, slice(h, rows))):
        real, imag = part[:, :, :h], part[:, :, h:]
        v_ref[:, :groups, lanes] = (real * twr[:, lanes] + imag * twi[:, lanes]).astype(BF16)
        v_ref[:, groups:, lanes] = (imag * twr[:, lanes] - real * twi[:, lanes]).astype(BF16)
    out = jnp.stack([dot(first_t_ref[...], v_ref[c]) for c in range(chans)], axis=0)
    return jnp.swapaxes(out.astype(BF16), 0, 1)


def forward_kernel(scale, *refs):
    arrived = refs[:4]
    x_ref, first_ref, first_t_ref, second_ref, twr_ref, twi_ref = refs[4:10]
    own_ref, other_ref, rest_ref, prod_ref, t_ref, v_ref, y_ref = refs[10:]
    rows = twr_ref.shape[1]
    h = rows // 2
    twr, twi = twr_ref[...], twi_ref[...]
    gather(lax.axis_index("context"), arrived, y_ref)
    gated = jnp.concatenate([y_ref[:, :, rows:], x_ref[:, :, rows:]], axis=2)
    taps, gated, delta = (
        spectrum(jnp.swapaxes(block, 0, 1), first_ref, second_ref, twr, twi, t_ref.at[s])
        for s, block in enumerate((y_ref[:, :, :rows], gated, x_ref[:, :, :rows]))
    )
    for parity in (0, 1):
        prod_ref[parity] = products(gated[parity], delta[parity], h, True)
    even, odd = (dot(products(gated[parity], taps[parity], h, False), second_ref[1, parity]) for parity in (0, 1))
    y_ref[:, :, :rows] = signal(scale, even, odd, first_t_ref, twr, twi, v_ref.at[0])
    even, odd = (dot(products(taps[parity], delta[parity], h, True), second_ref[1, parity]) for parity in (0, 1))
    back = signal(scale, even, odd, first_t_ref, twr, twi, v_ref.at[1])
    y_ref[:, :, rows:] = back[:, :, :h]
    rest_ref[...] = back[:, :, h:]
    halve(lax.axis_index("context"), y_ref, own_ref, other_ref)


def backward_kernel(
    scale, prod_ref, rest_ref, first_t_ref, second_ref, twr_ref, twi_ref, y_hbm, v_ref, y_ref, sems
):
    groups, chans, rows = y_ref.shape
    h = rows // 2
    twr, twi = twr_ref[...], twi_ref[...]
    copies = [
        pltpu.make_async_copy(rest_ref, y_hbm.at[:, :, pl.ds(rows, h)], sems.at[0]),
        pltpu.make_async_copy(y_ref, y_hbm.at[:, :, pl.ds(0, rows)], sems.at[1]),
    ]
    copies[0].start()
    even, odd = (dot(prod_ref[parity], second_ref[1, parity]) for parity in (0, 1))
    y_ref[...] = signal(scale, even, odd, first_t_ref, twr, twi, v_ref)
    copies[1].start()
    for copy in copies:
        copy.wait()


class Writer:
    def __init__(self, outs, held, sems):
        self.outs, self.held, self.sems, self.copies = outs, held, sems, []

    def put(self, i, p, block):
        step = self.held.shape[2]
        self.held[i, p] = block.astype(BF16)
        copy = pltpu.make_async_copy(self.held.at[i, p], self.outs[i].at[pl.ds(p * step, step)], self.sems.at[i, p])
        copy.start()
        self.copies.append(copy)

    def wait(self):
        for copy in self.copies:
            copy.wait()


def gate_kernel(*refs):
    arrived = refs[:4]
    y_ref, q_ref, k_ref, v_ref, og_ref, bias_ref, mixed_hbm, qg_hbm, kg_hbm, vg_hbm, fg_hbm, x_ref, held, sems = refs[4:]
    owners, chans, _ = x_ref.shape
    writer = Writer((mixed_hbm, qg_hbm, kg_hbm, vg_hbm, fg_hbm), held, sems)
    parts, step = held.shape[1:3]
    bias = bias_ref[...]

    def take(ref, p):
        return ref[:, :, p * step : (p + 1) * step].reshape(owners * chans, step).T

    for p in range(parts):
        writer.put(4, p, take(y_ref, p))
    gather(lax.axis_index("context"), arrived, x_ref)
    for p in range(parts):
        span = slice(p * step, (p + 1) * step)
        q, k, v, og = q_ref[span], k_ref[span], v_ref[span], og_ref[span]
        pre_gate = take(x_ref, p).astype(F32) + bias * (k * v).astype(F32)
        writer.put(0, p, q.astype(F32) * pre_gate)
        writer.put(1, p, og.astype(F32) * pre_gate)
        back = take((x_ref, y_ref)[p], parts)
        gated_grad = back.astype(F32) + bias * (og * q).astype(F32)
        writer.put(2, p, gated_grad * v.astype(F32))
        writer.put(3, p, gated_grad * k.astype(F32))
    writer.wait()


def local(q_gate, k_gate, v_input, filter_taps, skip_bias, out_grad):
    groups = lax.axis_size("context")
    rows, width = q_gate.shape
    chans = width // groups
    order = device_order(groups)
    seq = groups * rows
    scale = 2.0 / (2 * seq) / math.sqrt(seq)
    messages = jax.ShapeDtypeStruct((groups, 3 * chans, rows), BF16)
    whole = jax.ShapeDtypeStruct((rows, width), BF16)
    limit = pltpu.CompilerParams(vmem_limit_bytes=48 * 1024 * 1024)
    far = pl.BlockSpec(memory_space=pltpu.HBM)
    near = pl.BlockSpec(memory_space=pltpu.VMEM)

    def swap(block):
        return lax.all_to_all(
            block, "context", split_axis=0, concat_axis=0, tiled=True, axis_index_groups=[order]
        )

    block = (chans, rows + rows // 2)
    bins = (chans * groups, rows)

    def call(kernel, name, out_shape, scratch_shapes=(), weight=0, **more):
        if weight:
            more["cost_estimate"] = pl.CostEstimate(flops=weight, bytes_accessed=weight, transcendentals=0)
        return pl.pallas_call(
            kernel, out_shape=out_shape, scratch_shapes=list(scratch_shapes), compiler_params=limit, name=name, **more
        )

    def shape(*dims):
        return jax.ShapeDtypeStruct(dims, BF16)

    def travel(own, other, after, weight):
        other = send(other, 0, 0, 1)
        leaving = call(
            along_z_kernel,
            "along_z",
            [shape(2, 4, *own.shape[2:])] * 3,
            weight=weight,
            in_specs=[near] * 2 + [pl.BlockSpec(memory_space=pl.ANY)],
            out_specs=[near] * 3,
        )(own, other, after)
        arrived = [None] * 3
        for dz in ZORDER:
            arrived[dz - 1] = send(leaving[dz - 1], dz, 0, 0)
        kept, *leaving = call(along_x_kernel, "along_x", [shape(4, 2, *own.shape[2:])] * 4, weight=weight)(
            own, other, *arrived
        )
        return [kept] + [send(part, 0, dx, 0) for dx, part in enumerate(leaving, start=1)]

    first, first_t, second, twr, twi = make_tables(order, rows)
    def keep(*arrays):
        return [pltpu.with_memory_space_constraint(x, pltpu.HBM) for x in arrays]

    one, half = (chans, rows), (chans, rows // 2)
    own, other, rest = call(
        pack_early_kernel,
        "pack_early",
        [pltpu.VMEM((4, 4, *block), BF16)] * 2 + [pltpu.VMEM((groups, *half), BF16)],
        [pltpu.VMEM((3, rows, width), BF16), pltpu.VMEM((groups, *block), BF16), pltpu.SemaphoreType.DMA((3,))],
        in_specs=[far] * 3,
        out_specs=[near] * 3,
    )(*keep(filter_taps, k_gate, v_input))
    sent = call(
        pack_late_kernel,
        "pack_late",
        shape(groups, *block),
        [pltpu.VMEM((2, rows, width), BF16), pltpu.VMEM((groups, *one), BF16), pltpu.SemaphoreType.DMA((4,))],
        in_specs=[far] * 2 + [near],
        out_specs=far,
    )(*keep(q_gate, out_grad), rest)
    early = travel(own, other, sent, WEIGHT1)
    items = swap(sent)
    own, other, rest, crossed = call(
        functools.partial(forward_kernel, scale),
        "forward",
        [shape(4, 4, *block)] * 2
        + [shape(groups, *half), shape(2, *bins)],
        [
            pltpu.VMEM((3, 2, *bins), BF16),
            pltpu.VMEM((2, chans, 2 * groups, rows), BF16),
            pltpu.VMEM((groups, *block), BF16),
        ],
    )(*early, items, first, first_t, second, twr, twi)
    terms = call(
        functools.partial(backward_kernel, scale),
        "backward",
        shape(groups, *block),
        [
            pltpu.VMEM((chans, 2 * groups, rows), BF16),
            pltpu.VMEM((groups, *one), BF16),
            pltpu.SemaphoreType.DMA((2,)),
        ],
        in_specs=[near] * 6,
        out_specs=far,
    )(crossed, rest, first_t, second, twr, twi)
    arrived = travel(own, other, terms, WEIGHT)
    parts = 2
    return call(
        gate_kernel,
        "gate",
        [whole] * 5,
        [
            pltpu.VMEM((groups, *block), BF16),
            pltpu.VMEM((5, parts, rows // parts, width), BF16),
            pltpu.SemaphoreType.DMA((5, parts)),
        ],
        in_specs=[near] * 10,
        out_specs=[far] * 5,
    )(*arrived, swap(terms), q_gate, k_gate, v_input, out_grad, skip_bias[None, :])


def solution(mesh):
    spec = P("context", "tensor")
    return jax.shard_map(
        local,
        mesh=mesh,
        in_specs=(spec, spec, spec, spec, P("tensor"), spec),
        out_specs=(spec,) * 5,
        check_vma=False,
    )
```
